512 devices in a mesh: layer: 8 (over z), row: 8 (over x, core), col: 8 (over y).
Axes of the slice: x: 4, y: 8, z: 8, core: 2. Of those that a mesh axis runs over, the one named last changes fastest.
Arguments:
- c_states: float32 [8, 64, 64, 1024], P('layer', None, 'row', 'col'), may hold values from -6 to 6
- c_adjoints: float32 [8, 64, 64, 1024], P('layer', None, 'row', 'col'), may hold values from -6 to 6
- weights: bfloat16 [32, 64, 576], P('layer'), may hold values from -0.25 to 0.25
Outputs:
- new_states: float32 [8, 64, 64, 1024], P('layer', None, 'row', 'col')
- new_adjoints: float32 [8, 64, 64, 1024], P('layer', None, 'row', 'col')
- weight_grads: float32 [32, 64, 576], P('layer')
The draws below stay inside these ranges and needn't reach their ends.
All inputs are finite; a program needn't handle non-finite values.
Results may differ from the reference program's by a relative error of at most 0.006.
Values may be sent and summed in bfloat16 or wider, within the bound.
A program may use at most 64 MiB of HBM per device.

```python
import jax
import jax.numpy as jnp
from jax import lax

CH = 64
LG = 4
GROUPS = 8
LAYERS = 32
HH = 64
WW = 1024


def block_scale(rng, shape, pieces, low, largest):
    def one(dim, parts):
        heights = jax.random.uniform(jax.random.fold_in(jax.random.fold_in(rng, 6), dim), (parts,), jnp.float32, low / len(pieces), largest / len(pieces))
        return jnp.repeat(jnp.exp(heights), shape[dim] // parts).reshape((-1,) + (1,) * (len(shape) - dim - 1))

    gain = one(*pieces[0])
    for cut in pieces[1:]:
        gain = gain * one(*cut)
    return gain


def bell_draw(own_key, shape, spread, bound, pieces=(), kind=jnp.bfloat16):
    values = jax.random.normal(own_key, shape, jnp.float32) * spread
    if len(pieces) > 0:
        values = block_scale(own_key, shape, pieces, -0.22, 0.18) * values
    return jnp.clip(values, min=-bound, max=bound).astype(kind)


def setup_inputs(seed: int = 0) -> dict:
    key_of = jax.random.split(jax.random.key(seed), 4)
    return {
        "c_states": bell_draw(key_of[0], (GROUPS, CH, HH, WW), 1.0, 6.0, ((0, 8), (2, 8), (3, 8)), jnp.float32),
        "c_adjoints": bell_draw(key_of[1], (GROUPS, CH, HH, WW), 1.0, 6.0, ((0, 8), (2, 8), (3, 8)), jnp.float32),
        "weights": bell_draw(key_of[2], (LAYERS, CH, 9 * CH), (9 * CH) ** -0.5, 0.25, ((0, 8),)),
    }


step_size = 0.2


def patches(image):
    padded = jnp.pad(image, ((0, 0), (1, 1), (1, 1)))
    height = image.shape[1]
    width = image.shape[2]
    shifted = [padded[:, row_off:row_off + height, col_off:col_off + width] for row_off in range(3) for col_off in range(3)]
    return jnp.stack(shifted, 0).reshape(9 * image.shape[0], height * width)


def flipped(weight_mat):
    channels = weight_mat.shape[0]
    return jnp.transpose(weight_mat.reshape(channels, 9, channels)[:, ::-1, :], (2, 1, 0)).reshape(channels, 9 * channels)


def exact_dot(left_mat, right_mat):
    return jnp.dot(left_mat, right_mat, precision=lax.Precision.HIGHEST, preferred_element_type=jnp.float32)


def advance(state, weight_mat):
    active = state.astype(jnp.bfloat16)
    preact = jnp.dot(weight_mat, patches(active), preferred_element_type=jnp.float32).reshape(state.shape)
    return state + step_size * jnp.tanh(preact), active, preact


def reference(c_states, c_adjoints, weights):
    group_count = c_states.shape[0]
    channels = c_states.shape[1]
    shape = c_states.shape[1:]
    coarse = []
    group_end = []
    for group in range(group_count):
        state = c_states[group]
        for layer_pos in range(LG):
            state, _, _ = advance(state, weights[group * LG + layer_pos])
        group_end.append(state.reshape(channels, -1))
        summed = jnp.sum(weights[group * LG].astype(jnp.float32).reshape(channels, 9, channels), axis=1)
        coarse.append(jnp.eye(channels, dtype=jnp.float32) + step_size * summed)
    corrected = [c_states[0].reshape(channels, -1), group_end[0]]
    for group in range(1, group_count - 1):
        offset = group_end[group] - exact_dot(coarse[group], c_states[group].reshape(channels, -1))
        corrected.append(exact_dot(coarse[group], corrected[group]) + offset)
    grad_list = [None] * (group_count * LG)
    relaxed = []
    for group in range(group_count):
        state = corrected[group].reshape(shape)
        trail = []
        for layer_pos in range(LG):
            state, active, preact = advance(state, weights[group * LG + layer_pos])
            trail.append((active, preact))
        adjoint = c_adjoints[group]
        for layer_pos in reversed(range(LG)):
            active, preact = trail[layer_pos]
            slope = jnp.tanh(preact)
            source = (adjoint * step_size * (1.0 - slope * slope)).astype(jnp.bfloat16)
            grad_list[group * LG + layer_pos] = lax.dot_general(source.reshape(channels, -1), patches(active), (((1,), (1,)), ((), ())), preferred_element_type=jnp.float32)
            back = jnp.dot(flipped(weights[group * LG + layer_pos]), patches(source), preferred_element_type=jnp.float32)
            adjoint = adjoint + back.reshape(shape)
        relaxed.append(adjoint.reshape(channels, -1))
    lam = [None] * group_count
    lam[group_count - 1] = c_adjoints[group_count - 1].reshape(channels, -1)
    lam[group_count - 2] = relaxed[group_count - 1]
    for group in range(group_count - 2, 0, -1):
        transposed = coarse[group].T
        offset = relaxed[group] - exact_dot(transposed, c_adjoints[group].reshape(channels, -1))
        lam[group - 1] = exact_dot(transposed, lam[group]) + offset
    new_states = jnp.stack([item.reshape(shape) for item in corrected], 0)
    new_adjoints = jnp.stack([item.reshape(shape) for item in lam], 0)
    return new_states, new_adjoints, jnp.stack(grad_list, 0)
```

```python
import functools

import jax
import jax.numpy as jnp
from jax import lax
from jax.experimental import pallas as pl
from jax.experimental.pallas import tpu as pltpu
from jax.sharding import PartitionSpec as P

MESH = pl.DeviceIdType.MESH
F32 = jnp.float32
BF16 = jnp.bfloat16

CH = 64
LG = 4
TR = 8
TC = 128
NP = 8
HALO = 8
ST = TC + 2 * HALO
RW = TR + 2 * HALO
LEN = RW * ST
PAD = 256
WIDE = LEN + 2 * PAD
NEAR = ((0, -1), (0, 1), (-1, -1), (-1, 1), (1, -1), (1, 1))
PIECE = 144
step_size = 0.2


def span(halo):
    low, high = (HALO - halo) * ST, (HALO + TR + halo) * ST
    return low // 128 * 128, -(-high // 128) * 128


def chunks(bounds, size=256):
    low, high = bounds
    return [(at, min(size, high - at)) for at in range(low, high, size)]


def shifted(ref, rows, start, size):
    begin = start + PAD
    low = begin // 128 * 128
    off = begin - low
    if off == 0:
        return ref[rows, low : low + size]
    width = size + 128
    window = ref[rows, low : low + width]
    return pltpu.roll(window, width - off, 1)[:, :size]


def split3(matrix):
    high = matrix.astype(BF16)
    low = (matrix - high.astype(F32)).astype(BF16)
    return high, low


def body(
    x_in, q_in, w_ref, wall_ref, wback_ref,
    ns_ref, na_ref, wg_ref,
    x0, q0, n0, main_x, pack_x, main_q, pack_q, main_n, pack_n,
    rm_x, rp_x, rm_q, rp_q, rm_n, rp_n,
    amap, atmap, ga, gat, gc, gq, fb, gf, db, rd, dl, rl, gb, gg, eb, re,
    inside, own, xw, qw, yw, sa, ts, ss, so, sw,
    gpf, gpb, rr, hb, rc, pb, gall,
    send, recv,
):
    layer, row, col = (lax.axis_index(name) for name in ("layer", "row", "col"))
    finish = []
    counter = [0, 0]

    def slots(kind, count):
        first = counter[kind]
        counter[kind] += count
        return first

    def at(which, axis_name, by):
        return {axis_name: lax.rem(which + by + NP, NP)}

    def push(src, dst, send_at, recv_at, device):
        copy = pltpu.make_async_remote_copy(
            src_ref=src, dst_ref=dst, send_sem=send.at[send_at], recv_sem=recv.at[recv_at],
            device_id=device, device_id_type=MESH,
        )
        copy.start()
        return copy

    def arrived(dst, recv_at):
        pltpu.make_async_remote_copy(
            src_ref=dst, dst_ref=dst, send_sem=send.at[0], recv_sem=recv.at[recv_at],
            device_id={"layer": layer}, device_id_type=MESH,
        ).wait_recv()

    barrier = pltpu.get_barrier_semaphore()
    for by in range(1, NP):
        for which, name in ((layer, "layer"), (row, "row"), (col, "col")):
            pl.semaphore_signal(barrier, inc=1, device_id=at(which, name, by), device_id_type=MESH)
    for down, right in NEAR[2:]:
        pl.semaphore_signal(
            barrier, inc=1, device_id=at(row, "row", down) | at(col, "col", right), device_id_type=MESH
        )

    spot = lax.broadcasted_iota(jnp.int32, (TR * TC, 128), 0)
    lane = lax.broadcasted_iota(jnp.int32, (TR * TC, 128), 1)
    column, line = spot % TC, spot // TC
    picks = (lane < 64) & (column < HALO) & (lane == line * HALO + column)
    picks |= (lane >= 64) & (column >= TC - HALO) & (lane - 64 == line * HALO + column - (TC - HALO))
    edges = picks.astype(F32).astype(BF16)

    def pack_edges(main, pack):
        pack[...] = jnp.dot(main[...], edges, preferred_element_type=F32).astype(BF16)

    for r in range(TR):
        value = x_in[0, :, r, :]
        x0[r] = value
        main_x[:, r * TC : (r + 1) * TC] = value.astype(BF16)
    pack_edges(main_x, pack_x)

    def send_halo(main, pack, rows, rm, rp):
        first_s, first_r = slots(0, 8), slots(1, 8)
        width = rows * TC
        top, bottom = main.at[:, pl.ds(0, width)], main.at[:, pl.ds((TR - rows) * TC, width)]
        finish.append(push(
            bottom, rm.at[0, :, pl.ds((TR - rows) * TC, width)], first_s, first_r, at(row, "row", 1)
        ))
        finish.append(push(top, rm.at[1, :, pl.ds(0, width)], first_s + 1, first_r + 1, at(row, "row", -1)))
        for number, (down, right) in enumerate(NEAR):
            there = NEAR.index((-down, -right))
            device = at(col, "col", right)
            if down:
                device = device | at(row, "row", down)
            finish.append(push(pack, rp.at[there], first_s + 2 + number, first_r + 2 + there, device))

        def wait():
            arrived(rm.at[0, :, pl.ds((TR - rows) * TC, width)], first_r)
            arrived(rm.at[1, :, pl.ds(0, width)], first_r + 1)
            for number in range(6):
                arrived(rp.at[number], first_r + 2 + number)

        return wait

    def to_all(which, name, src_of, dst, dynamic=True):
        first_s, first_r = slots(0, NP), slots(1, NP)
        for by in range(1, NP):
            peer = lax.rem(which + by, NP)
            finish.append(push(
                src_of(peer), dst.at[which], first_s + by, first_r + which, {name: peer}
            ))

        def wait():
            for by in range(1, NP):
                peer = lax.rem(which + by, NP)
                arrived(dst.at[peer], first_r + peer)

        return wait

    pl.semaphore_wait(barrier, 3 * (NP - 1) + 4)
    wait_x = send_halo(main_x, pack_x, 4, rm_x, rp_x)

    tap_row = lax.broadcasted_iota(jnp.int32, (9 * CH, CH), 0)
    tap_col = lax.broadcasted_iota(jnp.int32, (9 * CH, CH), 1)
    fold = (tap_row % CH == tap_col).astype(F32).astype(BF16)
    fold_t = (
        lax.broadcasted_iota(jnp.int32, (CH, 9 * CH), 1) % CH == lax.broadcasted_iota(jnp.int32, (CH, 9 * CH), 0)
    ).astype(F32).astype(BF16)
    eye = (
        lax.broadcasted_iota(jnp.int32, (CH, CH), 0) == lax.broadcasted_iota(jnp.int32, (CH, CH), 1)
    ).astype(F32)
    summed = jnp.dot(w_ref[0], fold, preferred_element_type=F32)
    summed_t = lax.dot_general(fold_t, w_ref[0], (((1,), (1,)), ((), ())), preferred_element_type=F32)
    amap[...] = jnp.concatenate(split3(eye + step_size * summed), axis=1)
    atmap[...] = jnp.concatenate(split3(eye + step_size * summed_t), axis=1)
    wait_a = to_all(layer, "layer", lambda peer: amap, ga)
    wait_c = to_all(layer, "layer", lambda peer: x0.at[peer], gc)
    ga[layer] = amap[...]
    gat[layer] = atmap[...]
    gc[layer] = x0[layer]

    for r in range(TR):
        value = q_in[0, :, r, :]
        q0[r] = value
        main_q[:, r * TC : (r + 1) * TC] = value.astype(BF16)
    pack_edges(main_q, pack_q)
    wait_q = send_halo(main_q, pack_q, 4, rm_q, rp_q)

    place = lax.broadcasted_iota(jnp.int32, (8, WIDE), 1)
    lanes = place - PAD
    held = (lanes >= 0) & (lanes < LEN)
    safe = jnp.where(held, lanes, 0)
    r_at, c_at = safe // ST - HALO, safe % ST - HALO
    r_all, c_all = row * TR + r_at, col * TC + c_at
    ok = held & (r_all >= 0) & (r_all < NP * TR) & (c_all >= 0) & (c_all < NP * TC)
    inside[...] = ok.astype(F32)
    mine = held & (r_at >= 0) & (r_at < TR) & (c_at >= 0) & (c_at < TC)
    own[...] = mine.astype(F32)
    for ref in (xw, qw):
        ref[...] = jnp.zeros_like(ref)
    yw[...] = jnp.zeros_like(yw)
    so[...] = jnp.zeros_like(so)

    def assemble(ref, tile, rm, rp, halo):
        sides = ((rp[2], rp[3]), (rp[0], rp[1]), (rp[4], rp[5]))
        for line in range(HALO - halo, HALO + TR + halo):
            block, r = line // TR, line % TR
            start = PAD + line * ST
            if block == 1:
                main = tile[r]
            else:
                main = rm[block // 2, :, r * TC : (r + 1) * TC].astype(F32)
            left, right = sides[block]
            ref[:, start : start + ST] = jnp.concatenate(
                [
                    left[:, 64 + r * HALO : 64 + (r + 1) * HALO].astype(F32),
                    main,
                    right[:, r * HALO : (r + 1) * HALO].astype(F32),
                ],
                axis=1,
            )

    def spread(take, dst, bounds):
        for start, size in chunks(bounds):
            window = take(start - 128, size + 256)
            width = size + 256
            dst[0:CH, start : start + size] = pltpu.roll(window, 1, 1)[:, 128 : 128 + size].astype(BF16)
            dst[CH : 2 * CH, start : start + size] = window[:, 128 : 128 + size].astype(BF16)
            dst[2 * CH : 3 * CH, start : start + size] = pltpu.roll(window, width - 1, 1)[
                :, 128 : 128 + size
            ].astype(BF16)

    def multiply(matrix, src, bounds):
        for start, size in chunks(bounds):
            yw[:, PAD + start : PAD + start + size] = jnp.dot(
                matrix, src[:, start : start + size], preferred_element_type=F32
            )

    def gathered(start, size):
        total = yw[CH : 2 * CH, PAD + start : PAD + start + size]
        total += shifted(yw, slice(0, CH), start - ST, size)
        return total + shifted(yw, slice(2 * CH, 3 * CH), start + ST, size)

    def window_of(ref, start, size):
        return ref[:, PAD + start : PAD + start + size]

    def masked_state(start, size):
        return window_of(xw, start, size) * window_of(inside, start, size)[0:1]

    def forward(number, cols, slopes, halo):
        spread(masked_state, cols, span(halo + 1))
        multiply(wall_ref[number], cols, span(halo + 1))
        for start, size in chunks(span(halo)):
            bent = jnp.tanh(gathered(start, size))
            xw[:, PAD + start : PAD + start + size] += step_size * bent
            if slopes is not None:
                slopes[:, PAD + start : PAD + start + size] = step_size * (1.0 - bent * bent)

    def tile_row(ref, r):
        return shifted(ref, slice(0, CH), (HALO + r) * ST + HALO, TC)

    wait_x()
    assemble(xw, x0, rm_x, rp_x, 4)
    for number in range(LG):
        forward(number, sa.at[0], None, LG - 1 - number)
    for r in range(TR):
        fb[r] = (tile_row(xw, r) - x0[r]).astype(BF16)
    wait_f = to_all(layer, "layer", lambda peer: fb.at[peer], gf)
    gf[layer] = fb[layer]
    wait_a()
    wait_c()
    wait_f()

    def sweep(first, last, by, moves, guesses, maps, out, land, rest=None, rest_land=None):
        first_s, first_r = slots(0, NP), slots(1, NP)
        rest_s, rest_r = slots(0, NP), slots(1, NP)

        def hand(k, src, dst, s_at, r_at):
            @pl.when(layer != k)
            def _():
                push(src.at[k], dst.at[layer], s_at + k, r_at + layer, {"layer": k})

            @pl.when(layer == k)
            def _():
                dst[layer] = src[k]

        offset = None
        for k in range(first, last, by):
            change = moves[k].astype(F32) + (guesses[k] - guesses[k + by])
            if offset is not None:
                high, low = split3(offset)
                wide = maps[k]
                change += jnp.dot(
                    jnp.concatenate([wide, wide[:, :CH]], axis=1),
                    jnp.concatenate([high, high, low], axis=0),
                    preferred_element_type=F32,
                )
            offset = change
            high, low = split3(guesses[k + by] + offset)
            out[k + by] = high
            if rest is not None:
                rest[k + by] = low
            hand(k + by, out, land, first_s, first_r)
        if rest is not None:
            for k in range(first + by, last + by, by):
                hand(k, rest, rest_land, rest_s, rest_r)

        def wait(dst=land, r_at=first_r):
            @pl.when(layer != first)
            def _():
                for step in range(1, NP):
                    peer = lax.rem(layer + step, NP)
                    arrived(dst.at[peer], r_at + peer)

        def wait_rest():
            wait(rest_land, rest_r)

        def done():
            for src, dst, s_at, r_at in ((out, land, first_s, first_r), (rest, rest_land, rest_s, rest_r)):
                if src is None:
                    continue
                for k in range(first + by, last + by, by):

                    @pl.when(layer != k)
                    def _():
                        pltpu.make_async_remote_copy(
                            src_ref=src.at[k], dst_ref=dst.at[layer], send_sem=send.at[s_at + k],
                            recv_sem=recv.at[r_at + layer], device_id={"layer": k}, device_id_type=MESH,
                        ).wait_send()

        return wait, wait_rest, done

    wait_d, wait_rest, done_d = sweep(0, NP - 1, 1, gf, gc, ga, db, rd, dl, rl)

    @pl.when(layer == 0)
    def _():
        for r in range(TR):
            rd[r], rl[r] = split3(x0[r])

    wait_d()
    for r in range(TR):
        main_n[:, r * TC : (r + 1) * TC] = rd[r]
    pack_edges(main_n, pack_n)
    wait_n = send_halo(main_n, pack_n, TR, rm_n, rp_n)
    wait_at = to_all(layer, "layer", lambda peer: atmap, gat)
    wait_cq = to_all(layer, "layer", lambda peer: q0.at[peer], gq)
    gq[layer] = q0[layer]
    wait_rest()
    for r in range(TR):
        value = jnp.where(layer == 0, x0[r], rd[r].astype(F32) + rl[r].astype(F32))
        n0[r] = value
        ns_ref[0, :, r, :] = value
    wait_q()
    assemble(qw, q0, rm_q, rp_q, 4)

    wait_n()
    assemble(xw, n0, rm_n, rp_n, HALO)
    for number in range(LG):
        forward(number, sa.at[number], ts.at[number], 2 * LG - 1 - number)

    grad_low, grad_high = span(1)
    first_s_rr, first_r_rr = slots(0, NP), slots(1, NP)

    def source_of(number):
        def take(start, size):
            return (
                window_of(qw, start, size)
                * window_of(ts.at[number], start, size)
                * window_of(inside, start, size)[0:1]
            )

        return take

    for number in reversed(range(LG)):
        halo = number
        take = source_of(number)
        spread(take, ss, span(halo + 1))
        for start, size in chunks(span(0)):
            so[:, PAD + start : PAD + start + size] = take(start, size) * window_of(own, start, size)[0:1]
        for start, size in chunks((grad_low, grad_high)):
            to = start - grad_low
            sw[0:CH, to : to + size] = shifted(so, slice(0, CH), start + ST, size).astype(BF16)
            sw[CH : 2 * CH, to : to + size] = window_of(so, start, size).astype(BF16)
            sw[2 * CH : 3 * CH, to : to + size] = shifted(so, slice(0, CH), start - ST, size).astype(BF16)
        grad = lax.dot_general(
            sw[...], sa[number, :, grad_low:grad_high], (((1,), (1,)), ((), ())), preferred_element_type=F32
        )
        packed = jnp.concatenate(
            [grad[:, :128], jnp.concatenate([grad[:96, 128:192], grad[96:, 128:192]], axis=1)], axis=0
        )
        for half in range(2):
            piece = 2 * number + half
            gpf[piece] = packed[half * PIECE : (half + 1) * PIECE]
            gpb[piece] = packed[half * PIECE : (half + 1) * PIECE].astype(BF16)

            @pl.when(row != piece)
            def _():
                push(gpb.at[piece], rr.at[row], first_s_rr + piece, first_r_rr + row, {"row": piece})

        multiply(wback_ref[number], ss, span(halo + 1))
        for start, size in chunks(span(halo)):
            qw[:, PAD + start : PAD + start + size] += gathered(start, size)

    for r in range(TR):
        gb[r] = (tile_row(qw, r) - q0[r]).astype(BF16)
    wait_g = to_all(layer, "layer", lambda peer: gb.at[peer], gg)
    gg[layer] = gb[layer]
    wait_at()
    wait_cq()
    wait_g()
    wait_e, _, done_e = sweep(NP - 1, 0, -1, gg, gq, gat, eb, re)

    total = gpf[row]
    for by in range(1, NP):
        peer = lax.rem(row + by, NP)
        arrived(rr.at[peer], first_r_rr + peer)
        total += rr[peer].astype(F32)
    hb[...] = total.astype(BF16)
    wait_rc = to_all(col, "col", lambda peer: hb, rc)
    rc[col] = hb[...]

    @pl.when(layer == NP - 1)
    def _():
        for r in range(TR):
            na_ref[0, :, r, :] = q0[r]

    @pl.when(layer != NP - 1)
    def _():
        wait_e()
        for r in range(TR):
            na_ref[0, :, r, :] = re[r].astype(F32)

    wait_rc()
    total = rc[0].astype(F32)
    for k in range(1, NP):
        total += rc[k].astype(F32)
    pb[...] = total.astype(BF16)
    wait_all = to_all(row, "row", lambda peer: pb, gall)
    gall[row] = pb[...]
    wait_all()
    for number in range(LG):
        packed = jnp.concatenate([gall[2 * number], gall[2 * number + 1]], axis=0).astype(F32)
        rest = jnp.concatenate([packed[192:, :64], packed[192:, 64:]], axis=0)
        for r in range(3):
            wg_ref[number, :, r * 192 : (r + 1) * 192] = jnp.concatenate(
                [packed[r * CH : (r + 1) * CH], rest[r * CH : (r + 1) * CH]], axis=1
            )

    for copy in finish:
        copy.wait_send()
    done_d()
    done_e()
    for piece in range(NP):

        @pl.when(row != piece)
        def _():
            pltpu.make_async_remote_copy(
                src_ref=gpb.at[piece], dst_ref=rr.at[row], send_sem=send.at[first_s_rr + piece],
                recv_sem=recv.at[first_r_rr + row], device_id={"row": piece}, device_id_type=MESH,
            ).wait_send()


def local(c_states, c_adjoints, weights):
    vm = pltpu.VMEM
    tile = (TR, CH, TC)
    flat = (CH, TR * TC)
    scratch = [
        vm(tile, F32), vm(tile, F32), vm(tile, F32),
        vm(flat, BF16), vm((CH, 128), BF16), vm(flat, BF16), vm((CH, 128), BF16), vm(flat, BF16), vm((CH, 128), BF16),
        vm((2,) + flat, BF16), vm((6, CH, 128), BF16), vm((2,) + flat, BF16), vm((6, CH, 128), BF16),
        vm((2,) + flat, BF16), vm((6, CH, 128), BF16),
        vm((CH, 128), BF16), vm((CH, 128), BF16), vm((NP, CH, 128), BF16), vm((NP, CH, 128), BF16),
        vm(tile, F32), vm(tile, F32), vm(tile, BF16), vm(tile, BF16), vm(tile, BF16), vm(tile, BF16), vm(tile, BF16), vm(tile, BF16),
        vm(tile, BF16), vm(tile, BF16), vm(tile, BF16), vm(tile, BF16),
        vm((8, WIDE), F32), vm((8, WIDE), F32), vm((CH, WIDE), F32), vm((CH, WIDE), F32),
        vm((3 * CH, WIDE), F32), vm((LG, 3 * CH, LEN), BF16), vm((LG, CH, WIDE), F32),
        vm((3 * CH, LEN), BF16), vm((CH, WIDE), F32), vm((3 * CH, span(1)[1] - span(1)[0]), BF16),
        vm((NP, PIECE, 128), F32), vm((NP, PIECE, 128), BF16), vm((NP, PIECE, 128), BF16),
        vm((PIECE, 128), BF16), vm((NP, PIECE, 128), BF16), vm((PIECE, 128), BF16), vm((NP, PIECE, 128), BF16),
        pltpu.SemaphoreType.DMA((128,)), pltpu.SemaphoreType.DMA((128,)),
    ]
    taps = weights.reshape(LG, CH, 3, 3, CH)
    ahead = jnp.transpose(weights.reshape(LG, CH, 3, 3 * CH), (0, 2, 1, 3)).reshape(LG, 3 * CH, 3 * CH)
    back = jnp.transpose(taps[:, :, ::-1, ::-1, :], (0, 2, 4, 3, 1)).reshape(LG, 3 * CH, 3 * CH)
    return pl.pallas_call(
        body,
        out_shape=(
            jax.ShapeDtypeStruct(c_states.shape, F32),
            jax.ShapeDtypeStruct(c_states.shape, F32),
            jax.ShapeDtypeStruct(weights.shape, F32),
        ),
        in_specs=[pl.BlockSpec(memory_space=pltpu.VMEM)] * 5,
        out_specs=[pl.BlockSpec(memory_space=pltpu.VMEM)] * 3,
        scratch_shapes=scratch,
        compiler_params=pltpu.CompilerParams(
            collective_id=0, has_side_effects=True, vmem_limit_bytes=48 * 1024 * 1024
        ),
    )(c_states, c_adjoints, weights, ahead, back)


def solution(mesh):
    placed = (P("layer", None, "row", "col"), P("layer", None, "row", "col"), P("layer", None, None))
    return jax.shard_map(local, mesh=mesh, in_specs=placed, out_specs=placed, check_vma=False)
```

```python
import functools

import jax
import jax.numpy as jnp
from jax import lax
from jax.experimental import pallas as pl
from jax.experimental.pallas import tpu as pltpu
from jax.sharding import PartitionSpec as P

MESH = pl.DeviceIdType.MESH
F32 = jnp.float32
BF16 = jnp.bfloat16

CH = 64
LG = 4
TR = 8
TC = 128
NP = 8
HALO = 8
ST = TC + 2 * HALO
RW = TR + 2 * HALO
LEN = RW * ST
PAD = 256
WIDE = LEN + 2 * PAD
NEAR = ((0, -1), (0, 1), (-1, -1), (-1, 1), (1, -1), (1, 1))
PIECE = 144
step_size = 0.2


def span(halo):
    low, high = (HALO - halo) * ST, (HALO + TR + halo) * ST
    return low // 128 * 128, -(-high // 128) * 128


def chunks(bounds, size=256):
    low, high = bounds
    return [(at, min(size, high - at)) for at in range(low, high, size)]


def shifted(ref, rows, start, size):
    begin = start + PAD
    low = begin // 128 * 128
    off = begin - low
    if off == 0:
        return ref[rows, low : low + size]
    width = size + 128
    window = ref[rows, low : low + width]
    return pltpu.roll(window, width - off, 1)[:, :size]


def split3(matrix):
    high = matrix.astype(BF16)
    low = (matrix - high.astype(F32)).astype(BF16)
    return high, low


def body(
    x_in, q_in, w_ref,
    ns_ref, na_ref, wg_ref,
    x0, q0, n0, main_x, pack_x, main_q, pack_q, main_n, pack_n,
    rm_x, rp_x, rm_q, rp_q, rm_n, rp_n,
    amap, atmap, ga, gat, gc, gq, fb, gf, db, rd, dl, rl, gb, gg, eb, re,
    wall, wback, inside, own, xw, qw, yw, sa, ts, ss, so, sw,
    gpf, gpb, rr, hb, rc, pb, gall,
    send, recv,
):
    layer, row, col = (lax.axis_index(name) for name in ("layer", "row", "col"))
    finish = []
    counter = [0, 0]

    def slots(kind, count):
        first = counter[kind]
        counter[kind] += count
        return first

    def at(which, axis_name, by):
        return {axis_name: lax.rem(which + by + NP, NP)}

    def push(src, dst, send_at, recv_at, device):
        copy = pltpu.make_async_remote_copy(
            src_ref=src, dst_ref=dst, send_sem=send.at[send_at], recv_sem=recv.at[recv_at],
            device_id=device, device_id_type=MESH,
        )
        copy.start()
        return copy

    def arrived(dst, recv_at):
        pltpu.make_async_remote_copy(
            src_ref=dst, dst_ref=dst, send_sem=send.at[0], recv_sem=recv.at[recv_at],
            device_id={"layer": layer}, device_id_type=MESH,
        ).wait_recv()

    barrier = pltpu.get_barrier_semaphore()
    for by in range(1, NP):
        for which, name in ((layer, "layer"), (row, "row"), (col, "col")):
            pl.semaphore_signal(barrier, inc=1, device_id=at(which, name, by), device_id_type=MESH)
    for down, right in NEAR[2:]:
        pl.semaphore_signal(
            barrier, inc=1, device_id=at(row, "row", down) | at(col, "col", right), device_id_type=MESH
        )

    spot = lax.broadcasted_iota(jnp.int32, (TR * TC, 128), 0)
    lane = lax.broadcasted_iota(jnp.int32, (TR * TC, 128), 1)
    column, line = spot % TC, spot // TC
    picks = (lane < 64) & (column < HALO) & (lane == line * HALO + column)
    picks |= (lane >= 64) & (column >= TC - HALO) & (lane - 64 == line * HALO + column - (TC - HALO))
    edges = picks.astype(F32).astype(BF16)

    def pack_edges(main, pack):
        pack[...] = jnp.dot(main[...], edges, preferred_element_type=F32).astype(BF16)

    for r in range(TR):
        value = x_in[0, :, r, :]
        x0[r] = value
        main_x[:, r * TC : (r + 1) * TC] = value.astype(BF16)
    pack_edges(main_x, pack_x)

    def send_halo(main, pack, rows, rm, rp):
        first_s, first_r = slots(0, 8), slots(1, 8)
        width = rows * TC
        top, bottom = main.at[:, pl.ds(0, width)], main.at[:, pl.ds((TR - rows) * TC, width)]
        finish.append(push(
            bottom, rm.at[0, :, pl.ds((TR - rows) * TC, width)], first_s, first_r, at(row, "row", 1)
        ))
        finish.append(push(top, rm.at[1, :, pl.ds(0, width)], first_s + 1, first_r + 1, at(row, "row", -1)))
        for number, (down, right) in enumerate(NEAR):
            there = NEAR.index((-down, -right))
            device = at(col, "col", right)
            if down:
                device = device | at(row, "row", down)
            finish.append(push(pack, rp.at[there], first_s + 2 + number, first_r + 2 + there, device))

        def wait():
            arrived(rm.at[0, :, pl.ds((TR - rows) * TC, width)], first_r)
            arrived(rm.at[1, :, pl.ds(0, width)], first_r + 1)
            for number in range(6):
                arrived(rp.at[number], first_r + 2 + number)

        return wait

    def to_all(which, name, src_of, dst, dynamic=True):
        first_s, first_r = slots(0, NP), slots(1, NP)
        for by in range(1, NP):
            peer = lax.rem(which + by, NP)
            finish.append(push(
                src_of(peer), dst.at[which], first_s + by, first_r + which, {name: peer}
            ))

        def wait():
            for by in range(1, NP):
                peer = lax.rem(which + by, NP)
                arrived(dst.at[peer], first_r + peer)

        return wait

    pl.semaphore_wait(barrier, 3 * (NP - 1) + 4)
    wait_x = send_halo(main_x, pack_x, 4, rm_x, rp_x)

    tap_row = lax.broadcasted_iota(jnp.int32, (9 * CH, CH), 0)
    tap_col = lax.broadcasted_iota(jnp.int32, (9 * CH, CH), 1)
    fold = (tap_row % CH == tap_col).astype(F32).astype(BF16)
    fold_t = (
        lax.broadcasted_iota(jnp.int32, (CH, 9 * CH), 1) % CH == lax.broadcasted_iota(jnp.int32, (CH, 9 * CH), 0)
    ).astype(F32).astype(BF16)
    eye = (
        lax.broadcasted_iota(jnp.int32, (CH, CH), 0) == lax.broadcasted_iota(jnp.int32, (CH, CH), 1)
    ).astype(F32)
    summed = jnp.dot(w_ref[0], fold, preferred_element_type=F32)
    summed_t = lax.dot_general(fold_t, w_ref[0], (((1,), (1,)), ((), ())), preferred_element_type=F32)
    amap[...] = jnp.concatenate(split3(eye + step_size * summed), axis=1)
    atmap[...] = jnp.concatenate(split3(eye + step_size * summed_t), axis=1)
    wait_a = to_all(layer, "layer", lambda peer: amap, ga)
    wait_c = to_all(layer, "layer", lambda peer: x0.at[peer], gc)
    ga[layer] = amap[...]
    gat[layer] = atmap[...]
    gc[layer] = x0[layer]

    place = lax.broadcasted_iota(jnp.int32, (8, WIDE), 1)
    lanes = place - PAD
    held = (lanes >= 0) & (lanes < LEN)
    safe = jnp.where(held, lanes, 0)
    r_at, c_at = safe // ST - HALO, safe % ST - HALO
    r_all, c_all = row * TR + r_at, col * TC + c_at
    ok = held & (r_all >= 0) & (r_all < NP * TR) & (c_all >= 0) & (c_all < NP * TC)
    inside[...] = ok.astype(F32)
    mine = held & (r_at >= 0) & (r_at < TR) & (c_at >= 0) & (c_at < TC)
    own[...] = mine.astype(F32)
    xw[...] = jnp.zeros_like(xw)
    yw[...] = jnp.zeros_like(yw)
    for number in range(LG):
        for r in range(3):
            wall[number, r * CH : (r + 1) * CH, :] = w_ref[number, :, r * 192 : (r + 1) * 192]

    def assemble(ref, tile, rm, rp, halo):
        sides = ((rp[2], rp[3]), (rp[0], rp[1]), (rp[4], rp[5]))
        for line in range(HALO - halo, HALO + TR + halo):
            block, r = line // TR, line % TR
            start = PAD + line * ST
            if block == 1:
                main = tile[r]
            else:
                main = rm[block // 2, :, r * TC : (r + 1) * TC].astype(F32)
            left, right = sides[block]
            ref[:, start : start + ST] = jnp.concatenate(
                [
                    left[:, 64 + r * HALO : 64 + (r + 1) * HALO].astype(F32),
                    main,
                    right[:, r * HALO : (r + 1) * HALO].astype(F32),
                ],
                axis=1,
            )

    def spread(take, dst, bounds):
        for start, size in chunks(bounds, 512):
            width = size + 256
            window = take(start - 128, width).astype(BF16)
            dst[0:CH, start : start + size] = pltpu.roll(window[:, : size + 128], 1, 1)[:, 128 : 128 + size]
            dst[CH : 2 * CH, start : start + size] = window[:, 128 : 128 + size]
            dst[2 * CH : 3 * CH, start : start + size] = pltpu.roll(window[:, 128:], size + 127, 1)[:, :size]

    def multiply(matrix, src, bounds):
        for start, size in chunks(bounds):
            yw[:, PAD + start : PAD + start + size] = jnp.dot(
                matrix, src[:, start : start + size], preferred_element_type=F32
            )

    def gathered(start, size):
        total = yw[CH : 2 * CH, PAD + start : PAD + start + size]
        total += shifted(yw, slice(0, CH), start - ST, size)
        return total + shifted(yw, slice(2 * CH, 3 * CH), start + ST, size)

    def window_of(ref, start, size):
        return ref[:, PAD + start : PAD + start + size]

    def masked_state(start, size):
        return window_of(xw, start, size) * window_of(inside, start, size)[0:1]

    def forward(number, cols, slopes, halo):
        spread(masked_state, cols, span(halo + 1))
        multiply(wall[number], cols, span(halo + 1))
        for start, size in chunks(span(halo), 1024):
            bent = jnp.tanh(gathered(start, size))
            xw[:, PAD + start : PAD + start + size] += step_size * bent
            if slopes is not None:
                slopes[:, PAD + start : PAD + start + size] = step_size * (1.0 - bent * bent)

    def tile_row(ref, r):
        return shifted(ref, slice(0, CH), (HALO + r) * ST + HALO, TC)

    wait_x()
    assemble(xw, x0, rm_x, rp_x, 4)
    for number in range(LG):
        forward(number, sa.at[0], None, LG - 1 - number)
    for r in range(TR):
        fb[r] = (tile_row(xw, r) - x0[r]).astype(BF16)
    wait_f = to_all(layer, "layer", lambda peer: fb.at[peer], gf)
    gf[layer] = fb[layer]
    for r in range(TR):
        value = q_in[0, :, r, :]
        q0[r] = value
        main_q[:, r * TC : (r + 1) * TC] = value.astype(BF16)
    pack_edges(main_q, pack_q)
    wait_q = send_halo(main_q, pack_q, 4, rm_q, rp_q)

    qw[...] = jnp.zeros_like(qw)
    so[...] = jnp.zeros_like(so)
    same = (
        lax.broadcasted_iota(jnp.int32, (3 * CH, 3 * CH), 0) == lax.broadcasted_iota(jnp.int32, (3 * CH, 3 * CH), 1)
    ).astype(F32).astype(BF16)
    for number in range(LG):
        for r in range(3):
            turned = lax.dot_general(
                same, wall[number, r * CH : (r + 1) * CH, :], (((1,), (1,)), ((), ())), preferred_element_type=F32
            )
            wback[number, (2 - r) * CH : (3 - r) * CH, :] = jnp.concatenate(
                [turned[2 * CH :], turned[CH : 2 * CH], turned[:CH]], axis=1
            ).astype(BF16)
    wait_a()
    wait_c()
    wait_f()

    def sweep(first, last, by, moves, guesses, maps, out, land, rest=None, rest_land=None):
        first_s, first_r = slots(0, NP), slots(1, NP)
        rest_s, rest_r = slots(0, NP), slots(1, NP)

        def hand(k, src, dst, s_at, r_at):
            @pl.when(layer != k)
            def _():
                push(src.at[k], dst.at[layer], s_at + k, r_at + layer, {"layer": k})

            @pl.when(layer == k)
            def _():
                dst[layer] = src[k]

        offset = None
        for k in range(first, last, by):
            change = moves[k].astype(F32) + (guesses[k] - guesses[k + by])
            if offset is not None:
                high, low = split3(offset)
                wide = maps[k]
                change += jnp.dot(
                    jnp.concatenate([wide, wide[:, :CH]], axis=1),
                    jnp.concatenate([high, high, low], axis=0),
                    preferred_element_type=F32,
                )
            offset = change
            high, low = split3(guesses[k + by] + offset)
            out[k + by] = high
            if rest is not None:
                rest[k + by] = low
            hand(k + by, out, land, first_s, first_r)
        if rest is not None:
            for k in range(first + by, last + by, by):
                hand(k, rest, rest_land, rest_s, rest_r)

        def wait(dst=land, r_at=first_r):
            @pl.when(layer != first)
            def _():
                for step in range(1, NP):
                    peer = lax.rem(layer + step, NP)
                    arrived(dst.at[peer], r_at + peer)

        def wait_rest():
            wait(rest_land, rest_r)

        def done():
            for src, dst, s_at, r_at in ((out, land, first_s, first_r), (rest, rest_land, rest_s, rest_r)):
                if src is None:
                    continue
                for k in range(first + by, last + by, by):

                    @pl.when(layer != k)
                    def _():
                        pltpu.make_async_remote_copy(
                            src_ref=src.at[k], dst_ref=dst.at[layer], send_sem=send.at[s_at + k],
                            recv_sem=recv.at[r_at + layer], device_id={"layer": k}, device_id_type=MESH,
                        ).wait_send()

        return wait, wait_rest, done

    wait_d, wait_rest, done_d = sweep(0, NP - 1, 1, gf, gc, ga, db, rd, dl, rl)

    @pl.when(layer == 0)
    def _():
        for r in range(TR):
            rd[r], rl[r] = split3(x0[r])

    wait_d()
    for r in range(TR):
        main_n[:, r * TC : (r + 1) * TC] = rd[r]
    pack_edges(main_n, pack_n)
    wait_n = send_halo(main_n, pack_n, TR, rm_n, rp_n)
    wait_at = to_all(layer, "layer", lambda peer: atmap, gat)
    wait_cq = to_all(layer, "layer", lambda peer: q0.at[peer], gq)
    gq[layer] = q0[layer]
    wait_rest()
    for r in range(TR):
        value = jnp.where(layer == 0, x0[r], rd[r].astype(F32) + rl[r].astype(F32))
        n0[r] = value
        ns_ref[0, :, r, :] = value
    wait_q()
    assemble(qw, q0, rm_q, rp_q, 4)

    wait_n()
    assemble(xw, n0, rm_n, rp_n, HALO)
    for number in range(LG):
        forward(number, sa.at[number], ts.at[number], 2 * LG - 1 - number)

    grad_low, grad_high = span(1)
    first_s_rr, first_r_rr = slots(0, NP), slots(1, NP)

    def source_of(number):
        def take(start, size):
            return (
                window_of(qw, start, size)
                * window_of(ts.at[number], start, size)
                * window_of(inside, start, size)[0:1]
            )

        return take

    for number in reversed(range(LG)):
        halo = number
        take = source_of(number)
        spread(take, ss, span(halo + 1))
        for start, size in chunks(span(0)):
            so[:, PAD + start : PAD + start + size] = take(start, size) * window_of(own, start, size)[0:1]
        for start, size in chunks((grad_low, grad_high)):
            to = start - grad_low
            sw[0:CH, to : to + size] = shifted(so, slice(0, CH), start + ST, size).astype(BF16)
            sw[CH : 2 * CH, to : to + size] = window_of(so, start, size).astype(BF16)
            sw[2 * CH : 3 * CH, to : to + size] = shifted(so, slice(0, CH), start - ST, size).astype(BF16)
        grad = lax.dot_general(
            sw[...], sa[number, :, grad_low:grad_high], (((1,), (1,)), ((), ())), preferred_element_type=F32
        )
        packed = jnp.concatenate(
            [grad[:, :128], jnp.concatenate([grad[:96, 128:192], grad[96:, 128:192]], axis=1)], axis=0
        )
        for half in range(2):
            piece = 2 * number + half
            gpf[piece] = packed[half * PIECE : (half + 1) * PIECE]
            gpb[piece] = packed[half * PIECE : (half + 1) * PIECE].astype(BF16)

            @pl.when(row != piece)
            def _():
                push(gpb.at[piece], rr.at[row], first_s_rr + piece, first_r_rr + row, {"row": piece})

        multiply(wback[number], ss, span(halo + 1))
        for start, size in chunks(span(halo), 1024):
            qw[:, PAD + start : PAD + start + size] += gathered(start, size)

    for r in range(TR):
        gb[r] = (tile_row(qw, r) - q0[r]).astype(BF16)
    wait_g = to_all(layer, "layer", lambda peer: gb.at[peer], gg)
    gg[layer] = gb[layer]
    total = gpf[row]
    for by in range(1, NP):
        peer = lax.rem(row + by, NP)
        arrived(rr.at[peer], first_r_rr + peer)
        total += rr[peer].astype(F32)
    hb[...] = total.astype(BF16)
    wait_rc = to_all(col, "col", lambda peer: hb, rc)
    rc[col] = hb[...]

    wait_at()
    wait_cq()
    wait_g()
    wait_e, _, done_e = sweep(NP - 1, 0, -1, gg, gq, gat, eb, re)

    wait_rc()
    total = rc[0].astype(F32)
    for k in range(1, NP):
        total += rc[k].astype(F32)
    pb[...] = total.astype(BF16)
    wait_all = to_all(row, "row", lambda peer: pb, gall)
    gall[row] = pb[...]
    @pl.when(layer == NP - 1)
    def _():
        for r in range(TR):
            na_ref[0, :, r, :] = q0[r]

    @pl.when(layer != NP - 1)
    def _():
        wait_e()
        for r in range(TR):
            na_ref[0, :, r, :] = re[r].astype(F32)

    wait_all()
    for number in range(LG):
        packed = jnp.concatenate([gall[2 * number], gall[2 * number + 1]], axis=0).astype(F32)
        rest = jnp.concatenate([packed[192:, :64], packed[192:, 64:]], axis=0)
        for r in range(3):
            wg_ref[number, :, r * 192 : (r + 1) * 192] = jnp.concatenate(
                [packed[r * CH : (r + 1) * CH], rest[r * CH : (r + 1) * CH]], axis=1
            )

    for copy in finish:
        copy.wait_send()
    done_d()
    done_e()
    for piece in range(NP):

        @pl.when(row != piece)
        def _():
            pltpu.make_async_remote_copy(
                src_ref=gpb.at[piece], dst_ref=rr.at[row], send_sem=send.at[first_s_rr + piece],
                recv_sem=recv.at[first_r_rr + row], device_id={"row": piece}, device_id_type=MESH,
            ).wait_send()


def local(c_states, c_adjoints, weights):
    vm = pltpu.VMEM
    tile = (TR, CH, TC)
    flat = (CH, TR * TC)
    scratch = [
        vm(tile, F32), vm(tile, F32), vm(tile, F32),
        vm(flat, BF16), vm((CH, 128), BF16), vm(flat, BF16), vm((CH, 128), BF16), vm(flat, BF16), vm((CH, 128), BF16),
        vm((2,) + flat, BF16), vm((6, CH, 128), BF16), vm((2,) + flat, BF16), vm((6, CH, 128), BF16),
        vm((2,) + flat, BF16), vm((6, CH, 128), BF16),
        vm((CH, 128), BF16), vm((CH, 128), BF16), vm((NP, CH, 128), BF16), vm((NP, CH, 128), BF16),
        vm(tile, F32), vm(tile, F32), vm(tile, BF16), vm(tile, BF16), vm(tile, BF16), vm(tile, BF16), vm(tile, BF16), vm(tile, BF16),
        vm(tile, BF16), vm(tile, BF16), vm(tile, BF16), vm(tile, BF16),
        vm((LG, 3 * CH, 3 * CH), BF16), vm((LG, 3 * CH, 3 * CH), BF16),
        vm((8, WIDE), F32), vm((8, WIDE), F32), vm((CH, WIDE), F32), vm((CH, WIDE), F32),
        vm((3 * CH, WIDE), F32), vm((LG, 3 * CH, LEN), BF16), vm((LG, CH, WIDE), F32),
        vm((3 * CH, LEN), BF16), vm((CH, WIDE), F32), vm((3 * CH, span(1)[1] - span(1)[0]), BF16),
        vm((NP, PIECE, 128), F32), vm((NP, PIECE, 128), BF16), vm((NP, PIECE, 128), BF16),
        vm((PIECE, 128), BF16), vm((NP, PIECE, 128), BF16), vm((PIECE, 128), BF16), vm((NP, PIECE, 128), BF16),
        pltpu.SemaphoreType.DMA((128,)), pltpu.SemaphoreType.DMA((128,)),
    ]
    return pl.pallas_call(
        body,
        out_shape=(
            jax.ShapeDtypeStruct(c_states.shape, F32),
            jax.ShapeDtypeStruct(c_states.shape, F32),
            jax.ShapeDtypeStruct(weights.shape, F32),
        ),
        in_specs=[pl.BlockSpec(memory_space=pltpu.VMEM)] * 3,
        out_specs=[pl.BlockSpec(memory_space=pltpu.VMEM)] * 3,
        scratch_shapes=scratch,
        compiler_params=pltpu.CompilerParams(
            collective_id=0, has_side_effects=True, vmem_limit_bytes=48 * 1024 * 1024
        ),
    )(c_states, c_adjoints, weights)


def solution(mesh):
    placed = (P("layer", None, "row", "col"), P("layer", None, "row", "col"), P("layer", None, None))
    return jax.shard_map(local, mesh=mesh, in_specs=placed, out_specs=placed, check_vma=False)
```

```python
import functools

import jax
import jax.numpy as jnp
from jax import lax
from jax.experimental import pallas as pl
from jax.experimental.pallas import tpu as pltpu
from jax.sharding import PartitionSpec as P

MESH = pl.DeviceIdType.MESH
F32 = jnp.float32
BF16 = jnp.bfloat16

CH = 64
LG = 4
TR = 8
TC = 128
NP = 8
HALO = 8
RW = TR + 2 * HALO
MAIN = RW * TC
SIDE = RW * 2 * HALO
LEN = MAIN + SIDE
BLOCKS = RW // TR
NEAR = ((0, -1), (0, 1), (-1, -1), (-1, 1), (1, -1), (1, 1))
PIECE = 144
step_size = 0.2


def chunks(low, high, size):
    return [(at, min(size, high - at)) for at in range(low, high, size)]


def split3(matrix):
    high = matrix.astype(BF16)
    low = (matrix - high.astype(F32)).astype(BF16)
    return high, low


def body(
    x_hbm, q_hbm, w_hbm,
    ns_hbm, na_hbm, wg_hbm,
    ns_ref, na_ref, wg_ref, x_in, q_in, w_ref, x0, q0, n0, main_x, pack_x, main_q, pack_q, main_n, pack_n,
    rm_x, rp_x, rm_q, rp_q, rm_n, rp_n,
    amap, atmap, ga, gat, gc, gq, fb, gf, db, rd, dl, rl, gb, gg, eb, re,
    wall, wback, xw, qw, yw, sa, ts, ss, sw,
    gpf, gpb, rr, hb, share, common, mine, joined, pb, gall,
    send, recv, fetch,
):
    layer, row, col = (lax.axis_index(name) for name in ("layer", "row", "col"))
    finish = []
    counter = [0, 0]

    def slots(kind, count):
        first = counter[kind]
        counter[kind] += count
        return first

    def at(which, axis_name, by):
        return {axis_name: lax.rem(which + by + NP, NP)}

    def push(src, dst, send_at, recv_at, device):
        copy = pltpu.make_async_remote_copy(
            src_ref=src, dst_ref=dst, send_sem=send.at[send_at], recv_sem=recv.at[recv_at],
            device_id=device, device_id_type=MESH,
        )
        copy.start()
        return copy

    def arrived(dst, recv_at):
        pltpu.make_async_remote_copy(
            src_ref=dst, dst_ref=dst, send_sem=send.at[0], recv_sem=recv.at[recv_at],
            device_id={"layer": layer}, device_id_type=MESH,
        ).wait_recv()

    fetches = [
        pltpu.make_async_copy(src, dst, fetch.at[number])
        for number, (src, dst) in enumerate(((x_hbm, x_in), (w_hbm, w_ref), (q_hbm, q_in)))
    ]
    for copy in fetches:
        copy.start()

    barrier = pltpu.get_barrier_semaphore()
    for by in range(1, NP):
        for which, name in ((layer, "layer"), (row, "row"), (col, "col")):
            pl.semaphore_signal(barrier, inc=1, device_id=at(which, name, by), device_id_type=MESH)
    for down, right in NEAR[2:]:
        pl.semaphore_signal(
            barrier, inc=1, device_id=at(row, "row", down) | at(col, "col", right), device_id_type=MESH
        )

    spot = lax.broadcasted_iota(jnp.int32, (TR * TC, 128), 0)
    lane = lax.broadcasted_iota(jnp.int32, (TR * TC, 128), 1)
    column, line = spot % TC, spot // TC
    wanted = jnp.where(lane % 16 < HALO, TC - HALO + lane % 16, lane % 16 - HALO)
    picks = (lane // 16 == line) & (column == wanted)
    edges = picks.astype(F32).astype(BF16)

    def pack_edges(main, pack):
        pack[...] = jnp.dot(main[...], edges, preferred_element_type=F32).astype(BF16)

    fetches[0].wait()
    for r in range(TR):
        value = x_in[0, :, r, :]
        x0[r] = value
        main_x[:, r * TC : (r + 1) * TC] = value.astype(BF16)
    pack_edges(main_x, pack_x)

    def send_halo(main, pack, rows, rm, rp):
        first_s, first_r = slots(0, 8), slots(1, 8)
        width = rows * TC
        top, bottom = main.at[:, pl.ds(0, width)], main.at[:, pl.ds((TR - rows) * TC, width)]
        finish.append(push(
            bottom, rm.at[0, :, pl.ds((TR - rows) * TC, width)], first_s, first_r, at(row, "row", 1)
        ))
        finish.append(push(top, rm.at[1, :, pl.ds(0, width)], first_s + 1, first_r + 1, at(row, "row", -1)))
        for number, (down, right) in enumerate(NEAR):
            there = NEAR.index((-down, -right))
            device = at(col, "col", right)
            if down:
                device = device | at(row, "row", down)
            finish.append(push(pack, rp.at[there], first_s + 2 + number, first_r + 2 + there, device))

        def wait():
            arrived(rm.at[0, :, pl.ds((TR - rows) * TC, width)], first_r)
            arrived(rm.at[1, :, pl.ds(0, width)], first_r + 1)
            for number in range(6):
                arrived(rp.at[number], first_r + 2 + number)

        return wait

    def to_all(which, name, src_of, dst, dynamic=True):
        first_s, first_r = slots(0, NP), slots(1, NP)
        for by in range(1, NP):
            peer = lax.rem(which + by, NP)
            finish.append(push(
                src_of(peer), dst.at[which], first_s + by, first_r + which, {name: peer}
            ))

        def wait():
            for by in range(1, NP):
                peer = lax.rem(which + by, NP)
                arrived(dst.at[peer], first_r + peer)

        return wait

    pl.semaphore_wait(barrier, 3 * (NP - 1) + 4)
    wait_x = send_halo(main_x, pack_x, 4, rm_x, rp_x)

    tap_row = lax.broadcasted_iota(jnp.int32, (9 * CH, CH), 0)
    tap_col = lax.broadcasted_iota(jnp.int32, (9 * CH, CH), 1)
    fold = (tap_row % CH == tap_col).astype(F32).astype(BF16)
    fold_t = (
        lax.broadcasted_iota(jnp.int32, (CH, 9 * CH), 1) % CH == lax.broadcasted_iota(jnp.int32, (CH, 9 * CH), 0)
    ).astype(F32).astype(BF16)
    eye = (
        lax.broadcasted_iota(jnp.int32, (CH, CH), 0) == lax.broadcasted_iota(jnp.int32, (CH, CH), 1)
    ).astype(F32)
    fetches[1].wait()
    summed = jnp.dot(w_ref[0], fold, preferred_element_type=F32)
    summed_t = lax.dot_general(fold_t, w_ref[0], (((1,), (1,)), ((), ())), preferred_element_type=F32)
    amap[...] = jnp.concatenate(split3(eye + step_size * summed), axis=1)
    atmap[...] = jnp.concatenate(split3(eye + step_size * summed_t), axis=1)
    wait_a = to_all(layer, "layer", lambda peer: amap, ga)
    wait_c = to_all(layer, "layer", lambda peer: x0.at[peer], gc)
    ga[layer] = amap[...]
    gat[layer] = atmap[...]
    gc[layer] = x0[layer]

    block_ok = ((row > 0).astype(F32), None, (row < NP - 1).astype(F32))
    lane_in_row = lax.broadcasted_iota(jnp.int32, (1, 128), 1) % 16
    side_ok = jnp.where(lane_in_row < HALO, (col > 0).astype(F32), (col < NP - 1).astype(F32))
    lane_at = lax.broadcasted_iota(jnp.int32, (CH, 128), 1)
    lane_bf = lane_at.astype(F32).astype(BF16)
    lane16_bf = (lane_at % 16).astype(F32).astype(BF16)
    last_lane, first_lane = lane_bf == 127, lane_bf == 0
    left_end, right_end = lane16_bf == HALO - 1, lane16_bf == HALO
    o_row = lax.broadcasted_iota(jnp.int32, (128, TR * TC), 0)
    o_lane = lax.broadcasted_iota(jnp.int32, (128, TR * TC), 1)
    outward = (((o_lane % TC == 0) & (o_row == o_lane // TC * 16 + 7)) | ((o_lane % TC == 127) & (o_row == o_lane // TC * 16 + 8))).astype(F32).astype(BF16)
    pick0 = (lane_at == 0).astype(F32).astype(BF16)
    pick1 = (lane_at == 127).astype(F32).astype(BF16)
    keep0 = (lane_at != 0).astype(F32).astype(BF16)
    keep1 = (lane_at != 127).astype(F32).astype(BF16)
    on_left = lane_at % 16 < HALO
    for number in range(LG):
        for r in range(3):
            wall[number, r * CH : (r + 1) * CH, :] = w_ref[number, :, r * 192 : (r + 1) * 192]

    def assemble(ref, tile, rm, rp, halo):
        sides = ((2, 3), (0, 1), (4, 5))
        for line in range(HALO - halo, HALO + TR + halo):
            block, r = line // TR, line % TR
            main = tile[r] if block == 1 else rm[block // 2, :, r * TC : (r + 1) * TC].astype(F32)
            ref[:, line * TC : (line + 1) * TC] = main
        for block, (left, right) in enumerate(sides):
            start = MAIN + block * 128
            ref[:, start : start + 128] = jnp.where(on_left, rp[left].astype(F32), rp[right].astype(F32))

    def spread(take, dst, low, high):
        def put(start, values):
            for s, value in enumerate(values):
                dst[s * CH : (s + 1) * CH, start : start + 128] = value

        for block in range(BLOCKS):
            ok = block_ok[block]
            side = take(MAIN + block * 128) * side_ok
            side = (side if ok is None else side * ok).astype(BF16)
            crossing = jnp.zeros((CH, 128), BF16)
            arounds = jnp.dot(side, outward, preferred_element_type=F32).astype(BF16)
            for r in range(TR):
                line = block * TR + r
                if not low <= line < high:
                    continue
                main = take(line * TC)
                main = (main if ok is None else main * ok).astype(BF16)
                put(
                    line * TC,
                    (
                        pltpu.roll(main, 1, 1) * keep0 + arounds[:, r * 128 : (r + 1) * 128] * pick0,
                        main,
                        pltpu.roll(main, 127, 1) * keep1 + arounds[:, r * 128 : (r + 1) * 128] * pick1,
                    ),
                )
                beside = pltpu.roll(main, (16 * r + 8) % 128, 1)
                here = (lane_bf == 16 * r + 7) | (lane_bf == 16 * r + 8)
                crossing = jnp.where(here, beside, crossing)
            put(
                MAIN + block * 128,
                (
                    pltpu.roll(jnp.where(left_end, crossing, side), 1, 1),
                    side,
                    pltpu.roll(jnp.where(right_end, crossing, side), 127, 1),
                ),
            )

    def multiply(matrix, src, low, high):
        for start, size in chunks(low * TC, high * TC, 256) + chunks(MAIN, LEN, 256):
            yw[:, start : start + size] = jnp.dot(matrix, src[:, start : start + size], preferred_element_type=F32)

    def gathered(low, high):
        for start, size in chunks(low * TC, high * TC, 256):
            yield (
                start,
                size,
                yw[:CH, start - TC : start - TC + size]
                + yw[CH : 2 * CH, start : start + size]
                + yw[2 * CH :, start + TC : start + TC + size],
            )
        yield (
            MAIN,
            SIDE,
            pltpu.roll(yw[:CH, MAIN:], 16, 1) + yw[CH : 2 * CH, MAIN:] + pltpu.roll(yw[2 * CH :, MAIN:], SIDE - 16, 1),
        )

    def forward(number, cols, slopes, halo):
        low, high = HALO - halo, HALO + TR + halo
        spread(lambda start: xw[:, start : start + 128], cols, low - 1, high + 1)
        multiply(wall[number], cols, low - 1, high + 1)
        for start, size, total in gathered(low, high):
            bent = jnp.tanh(total)
            xw[:, start : start + size] += step_size * bent
            if slopes is not None:
                slopes[:, start : start + size] = step_size * (1.0 - bent * bent)

    def tile_row(ref, r):
        return ref[:, (HALO + r) * TC : (HALO + r + 1) * TC]

    wait_x()
    assemble(xw, x0, rm_x, rp_x, 4)
    for number in range(LG):
        forward(number, sa.at[0], None, LG - 1 - number)
    for r in range(TR):
        fb[r] = (tile_row(xw, r) - x0[r]).astype(BF16)
    wait_f = to_all(layer, "layer", lambda peer: fb.at[peer], gf)
    gf[layer] = fb[layer]
    fetches[2].wait()
    for r in range(TR):
        value = q_in[0, :, r, :]
        q0[r] = value
        main_q[:, r * TC : (r + 1) * TC] = value.astype(BF16)
    pack_edges(main_q, pack_q)
    wait_q = send_halo(main_q, pack_q, 4, rm_q, rp_q)

    sw[...] = jnp.zeros_like(sw)
    same = (
        lax.broadcasted_iota(jnp.int32, (3 * CH, 3 * CH), 0) == lax.broadcasted_iota(jnp.int32, (3 * CH, 3 * CH), 1)
    ).astype(F32).astype(BF16)
    for number in range(LG):
        for r in range(3):
            turned = lax.dot_general(
                same, wall[number, r * CH : (r + 1) * CH, :], (((1,), (1,)), ((), ())), preferred_element_type=F32
            )
            wback[number, (2 - r) * CH : (3 - r) * CH, :] = jnp.concatenate(
                [turned[2 * CH :], turned[CH : 2 * CH], turned[:CH]], axis=1
            ).astype(BF16)
    wait_a()
    wait_c()
    wait_f()

    def sweep(first, last, by, moves, guesses, maps, out, land, rest=None, rest_land=None):
        first_s, first_r = slots(0, NP), slots(1, NP)
        rest_s, rest_r = slots(0, NP), slots(1, NP)

        def hand(k, src, dst, s_at, r_at):
            @pl.when(layer != k)
            def _():
                push(src.at[k], dst.at[layer], s_at + k, r_at + layer, {"layer": k})

            @pl.when(layer == k)
            def _():
                dst[layer] = src[k]

        offset = None
        for k in range(first, last, by):
            change = moves[k].astype(F32) + (guesses[k] - guesses[k + by])
            if offset is not None:
                high, low = split3(offset)
                wide = maps[k]
                change += jnp.dot(
                    jnp.concatenate([wide, wide[:, :CH]], axis=1),
                    jnp.concatenate([high, high, low], axis=0),
                    preferred_element_type=F32,
                )
            offset = change
            high, low = split3(guesses[k + by] + offset)
            out[k + by] = high
            if rest is not None:
                rest[k + by] = low
            hand(k + by, out, land, first_s, first_r)
        if rest is not None:
            for k in range(first + by, last + by, by):
                hand(k, rest, rest_land, rest_s, rest_r)

        def wait(dst=land, r_at=first_r):
            @pl.when(layer != first)
            def _():
                for step in range(1, NP):
                    peer = lax.rem(layer + step, NP)
                    arrived(dst.at[peer], r_at + peer)

        def wait_rest():
            wait(rest_land, rest_r)

        def done():
            for src, dst, s_at, r_at in ((out, land, first_s, first_r), (rest, rest_land, rest_s, rest_r)):
                if src is None:
                    continue
                for k in range(first + by, last + by, by):

                    @pl.when(layer != k)
                    def _():
                        pltpu.make_async_remote_copy(
                            src_ref=src.at[k], dst_ref=dst.at[layer], send_sem=send.at[s_at + k],
                            recv_sem=recv.at[r_at + layer], device_id={"layer": k}, device_id_type=MESH,
                        ).wait_send()

        return wait, wait_rest, done

    wait_d, wait_rest, done_d = sweep(0, NP - 1, 1, gf, gc, ga, db, rd, dl, rl)

    @pl.when(layer == 0)
    def _():
        for r in range(TR):
            rd[r], rl[r] = split3(x0[r])

    wait_d()
    for r in range(TR):
        main_n[:, r * TC : (r + 1) * TC] = rd[r]
    pack_edges(main_n, pack_n)
    wait_n = send_halo(main_n, pack_n, TR, rm_n, rp_n)
    wait_at = to_all(layer, "layer", lambda peer: atmap, gat)
    wait_cq = to_all(layer, "layer", lambda peer: q0.at[peer], gq)
    gq[layer] = q0[layer]
    wait_rest()
    for r in range(TR):
        value = jnp.where(layer == 0, x0[r], rd[r].astype(F32) + rl[r].astype(F32))
        n0[r] = value
        ns_ref[0, :, r, :] = value
    stores = [pltpu.make_async_copy(ns_ref, ns_hbm, fetch.at[3])]
    stores[0].start()
    wait_q()
    assemble(qw, q0, rm_q, rp_q, 4)

    wait_n()
    assemble(xw, n0, rm_n, rp_n, HALO)
    for number in range(LG):
        forward(number, sa.at[number], ts.at[number], 2 * LG - 1 - number)

    first_s_rr, first_r_rr = slots(0, NP), slots(1, NP)

    for number in reversed(range(LG)):
        low, high = HALO - number, HALO + TR + number
        slopes = ts.at[number]
        spread(lambda start: qw[:, start : start + 128] * slopes[:, start : start + 128], ss, low - 1, high + 1)
        for r in range(3):
            start = r * TC
            sw[r * CH : (r + 1) * CH, start : start + TR * TC] = ss[CH : 2 * CH, HALO * TC : (HALO + TR) * TC]
        grad = lax.dot_general(
            sw[...], sa[number, :, (HALO - 1) * TC : (HALO + TR + 1) * TC], (((1,), (1,)), ((), ())),
            preferred_element_type=F32,
        )
        packed = jnp.concatenate(
            [grad[:, :128], jnp.concatenate([grad[:96, 128:192], grad[96:, 128:192]], axis=1)], axis=0
        )
        for half in range(2):
            piece = 2 * number + half
            gpf[piece] = packed[half * PIECE : (half + 1) * PIECE]
            gpb[piece] = packed[half * PIECE : (half + 1) * PIECE].astype(BF16)

            @pl.when(row != piece)
            def _():
                push(gpb.at[piece], rr.at[row], first_s_rr + piece, first_r_rr + row, {"row": piece})

        multiply(wback[number], ss, low - 1, high + 1)
        for start, size, total in gathered(low, high):
            qw[:, start : start + size] += total

    for r in range(TR):
        gb[r] = (tile_row(qw, r) - q0[r]).astype(BF16)
    wait_g = to_all(layer, "layer", lambda peer: gb.at[peer], gg)
    gg[layer] = gb[layer]
    total = gpf[row]
    for by in range(1, NP):
        peer = lax.rem(row + by, NP)
        arrived(rr.at[peer], first_r_rr + peer)
        total += rr[peer].astype(F32)
    for k in range(NP + 1):
        hb[k] = total[16 * k : 16 * (k + 1)].astype(BF16)
    wait_share = to_all(col, "col", lambda peer: hb.at[peer], share)
    wait_rest = to_all(col, "col", lambda peer: hb.at[NP], common)
    share[col] = hb[col]
    common[col] = hb[NP]

    def added(parts):
        sum_of = parts[0].astype(F32)
        for k in range(1, NP):
            sum_of += parts[k].astype(F32)
        return sum_of.astype(BF16)

    wait_share()
    mine[...] = added(share)
    wait_mine = to_all(col, "col", lambda peer: mine, joined)
    joined[col] = mine[...]
    wait_at()
    wait_cq()
    wait_g()
    wait_e, _, done_e = sweep(NP - 1, 0, -1, gg, gq, gat, eb, re)

    wait_rest()
    wait_mine()
    pb[NP] = added(common)
    for k in range(NP):
        pb[k] = joined[k]
    wait_all = to_all(row, "row", lambda peer: pb, gall)
    gall[row] = pb[...]
    @pl.when(layer == NP - 1)
    def _():
        for r in range(TR):
            na_ref[0, :, r, :] = q0[r]

    @pl.when(layer != NP - 1)
    def _():
        wait_e()
        for r in range(TR):
            na_ref[0, :, r, :] = re[r].astype(F32)

    stores.append(pltpu.make_async_copy(na_ref, na_hbm, fetch.at[4]))
    stores[1].start()

    wait_all()
    for number in range(LG):
        packed = jnp.concatenate(
            [gall[2 * number + half, k] for half in range(2) for k in range(NP + 1)], axis=0
        ).astype(F32)
        rest = jnp.concatenate([packed[192:, :64], packed[192:, 64:]], axis=0)
        for r in range(3):
            wg_ref[number, :, r * 192 : (r + 1) * 192] = jnp.concatenate(
                [packed[r * CH : (r + 1) * CH], rest[r * CH : (r + 1) * CH]], axis=1
            )
        stores.append(pltpu.make_async_copy(wg_ref.at[number], wg_hbm.at[number], fetch.at[5 + number]))
        stores[-1].start()

    for copy in stores:
        copy.wait()
    for copy in finish:
        copy.wait_send()
    done_d()
    done_e()
    for piece in range(NP):

        @pl.when(row != piece)
        def _():
            pltpu.make_async_remote_copy(
                src_ref=gpb.at[piece], dst_ref=rr.at[row], send_sem=send.at[first_s_rr + piece],
                recv_sem=recv.at[first_r_rr + row], device_id={"row": piece}, device_id_type=MESH,
            ).wait_send()


def place_results(*refs):
    copies = [pltpu.make_async_copy(refs[k], refs[3 + k], refs[6].at[k]) for k in range(3)]
    for copy in copies:
        copy.start()
    for copy in copies:
        copy.wait()


def local(c_states, c_adjoints, weights):
    vm = pltpu.VMEM
    tile = (TR, CH, TC)
    flat = (CH, TR * TC)
    scratch = [
        vm(c_states.shape, F32), vm(c_states.shape, F32), vm(weights.shape, F32),
        vm(c_states.shape, F32), vm(c_states.shape, F32), vm(weights.shape, BF16),
        vm(tile, F32), vm(tile, F32), vm(tile, F32),
        vm(flat, BF16), vm((CH, 128), BF16), vm(flat, BF16), vm((CH, 128), BF16), vm(flat, BF16), vm((CH, 128), BF16),
        vm((2,) + flat, BF16), vm((6, CH, 128), BF16), vm((2,) + flat, BF16), vm((6, CH, 128), BF16),
        vm((2,) + flat, BF16), vm((6, CH, 128), BF16),
        vm((CH, 128), BF16), vm((CH, 128), BF16), vm((NP, CH, 128), BF16), vm((NP, CH, 128), BF16),
        vm(tile, F32), vm(tile, F32), vm(tile, BF16), vm(tile, BF16), vm(tile, BF16), vm(tile, BF16), vm(tile, BF16), vm(tile, BF16),
        vm(tile, BF16), vm(tile, BF16), vm(tile, BF16), vm(tile, BF16),
        vm((LG, 3 * CH, 3 * CH), BF16), vm((LG, 3 * CH, 3 * CH), BF16),
        vm((CH, LEN), F32), vm((CH, LEN), F32),
        vm((3 * CH, LEN), F32), vm((LG, 3 * CH, LEN), BF16), vm((LG, CH, LEN), F32),
        vm((3 * CH, LEN), BF16), vm((3 * CH, (TR + 2) * TC), BF16),
        vm((NP, PIECE, 128), F32), vm((NP, PIECE, 128), BF16), vm((NP, PIECE, 128), BF16),
        vm((NP + 1, 16, 128), BF16), vm((NP, 16, 128), BF16), vm((NP, 16, 128), BF16), vm((16, 128), BF16),
        vm((NP, 16, 128), BF16), vm((NP + 1, 16, 128), BF16), vm((NP, NP + 1, 16, 128), BF16),
        pltpu.SemaphoreType.DMA((160,)), pltpu.SemaphoreType.DMA((160,)), pltpu.SemaphoreType.DMA((5 + LG,)),
    ]
    results = pl.pallas_call(
        body,
        out_shape=(
            jax.ShapeDtypeStruct(c_states.shape, F32),
            jax.ShapeDtypeStruct(c_states.shape, F32),
            jax.ShapeDtypeStruct(weights.shape, F32),
        ),
        in_specs=[pl.BlockSpec(memory_space=pltpu.HBM)] * 3,
        out_specs=[pl.BlockSpec(memory_space=pltpu.HBM)] * 3,
        scratch_shapes=scratch,
        compiler_params=pltpu.CompilerParams(
            collective_id=0, has_side_effects=True, vmem_limit_bytes=60 * 1024 * 1024
        ),
    )(c_states, c_adjoints, weights)
    return pl.pallas_call(
        place_results,
        out_shape=tuple(jax.ShapeDtypeStruct(value.shape, F32) for value in results),
        in_specs=[pl.BlockSpec(memory_space=pltpu.HBM)] * 3,
        out_specs=[pl.BlockSpec(memory_space=pltpu.HBM)] * 3,
        scratch_shapes=[pltpu.SemaphoreType.DMA((3,))],
        compiler_params=pltpu.CompilerParams(vmem_limit_bytes=60 * 1024 * 1024),
    )(*results)


def solution(mesh):
    placed = (P("layer", None, "row", "col"), P("layer", None, "row", "col"), P("layer", None, None))
    return jax.shard_map(local, mesh=mesh, in_specs=placed, out_specs=placed, check_vma=False)
```

```python
import functools

import jax
import jax.numpy as jnp
from jax import lax
from jax.experimental import pallas as pl
from jax.experimental.pallas import tpu as pltpu
from jax.sharding import PartitionSpec as P

MESH = pl.DeviceIdType.MESH
F32 = jnp.float32
BF16 = jnp.bfloat16

CH = 64
LG = 4
TR = 8
TC = 128
NP = 8
HALO = 8
RW = TR + 2 * HALO
MAIN = RW * TC
SIDE = RW * 2 * HALO
LEN = MAIN + SIDE
BLOCKS = RW // TR
NEAR = ((0, -1), (0, 1), (-1, -1), (-1, 1), (1, -1), (1, 1))
PIECE = 144
step_size = 0.2


def chunks(low, high, size):
    return [(at, min(size, high - at)) for at in range(low, high, size)]


def split3(matrix):
    high = matrix.astype(BF16)
    low = (matrix - high.astype(F32)).astype(BF16)
    return high, low


def body(
    x_hbm, q_hbm, w_hbm,
    ns_hbm, na_hbm, wg_hbm,
    ns_ref, na_ref, wg_ref, x_in, q_in, w_ref, x0, q0, n0, main_x, pack_x, main_q, pack_q, main_n, pack_n,
    rm_x, rp_x, rm_q, rp_q, rm_n, rp_n,
    amap, atmap, ga, gat, gc, gq, fb, gf, db, rd, dl, rl, gb, gg, eb, re,
    wall, wback, xw, qw, yw, sa, ts, ss, sw,
    gpf, gpb, rr, hb, share, common, mine, joined, pb, gall,
    send, recv, fetch,
):
    layer, row, col = (lax.axis_index(name) for name in ("layer", "row", "col"))
    finish = []
    counter = [0, 0]

    def slots(kind, count):
        first = counter[kind]
        counter[kind] += count
        return first

    def at(which, axis_name, by):
        return {axis_name: lax.rem(which + by + NP, NP)}

    def push(src, dst, send_at, recv_at, device):
        copy = pltpu.make_async_remote_copy(
            src_ref=src, dst_ref=dst, send_sem=send.at[send_at], recv_sem=recv.at[recv_at],
            device_id=device, device_id_type=MESH,
        )
        copy.start()
        return copy

    def arrived(dst, recv_at):
        pltpu.make_async_remote_copy(
            src_ref=dst, dst_ref=dst, send_sem=send.at[0], recv_sem=recv.at[recv_at],
            device_id={"layer": layer}, device_id_type=MESH,
        ).wait_recv()

    fetches = [
        pltpu.make_async_copy(src, dst, fetch.at[number])
        for number, (src, dst) in enumerate(((x_hbm, x_in), (w_hbm, w_ref), (q_hbm, q_in)))
    ]
    for copy in fetches:
        copy.start()

    barrier = pltpu.get_barrier_semaphore()
    for by in range(1, NP):
        for which, name in ((layer, "layer"), (row, "row"), (col, "col")):
            pl.semaphore_signal(barrier, inc=1, device_id=at(which, name, by), device_id_type=MESH)
    for down, right in NEAR[2:]:
        pl.semaphore_signal(
            barrier, inc=1, device_id=at(row, "row", down) | at(col, "col", right), device_id_type=MESH
        )

    spot = lax.broadcasted_iota(jnp.int32, (TR * TC, 128), 0)
    lane = lax.broadcasted_iota(jnp.int32, (TR * TC, 128), 1)
    column, line = spot % TC, spot // TC
    wanted = jnp.where(lane % 16 < HALO, TC - HALO + lane % 16, lane % 16 - HALO)
    picks = (lane // 16 == line) & (column == wanted)
    edges = picks.astype(F32).astype(BF16)

    def pack_edges(main, pack):
        pack[...] = jnp.dot(main[...], edges, preferred_element_type=F32).astype(BF16)

    fetches[0].wait()
    for r in range(TR):
        value = x_in[0, :, r, :]
        x0[r] = value
        main_x[:, r * TC : (r + 1) * TC] = value.astype(BF16)
    pack_edges(main_x, pack_x)

    def send_halo(main, pack, rows, rm, rp):
        first_s, first_r = slots(0, 8), slots(1, 8)
        width = rows * TC
        top, bottom = main.at[:, pl.ds(0, width)], main.at[:, pl.ds((TR - rows) * TC, width)]
        finish.append(push(
            bottom, rm.at[0, :, pl.ds((TR - rows) * TC, width)], first_s, first_r, at(row, "row", 1)
        ))
        finish.append(push(top, rm.at[1, :, pl.ds(0, width)], first_s + 1, first_r + 1, at(row, "row", -1)))
        for number, (down, right) in enumerate(NEAR):
            there = NEAR.index((-down, -right))
            device = at(col, "col", right)
            if down:
                device = device | at(row, "row", down)
            finish.append(push(pack, rp.at[there], first_s + 2 + number, first_r + 2 + there, device))

        def wait():
            arrived(rm.at[0, :, pl.ds((TR - rows) * TC, width)], first_r)
            arrived(rm.at[1, :, pl.ds(0, width)], first_r + 1)
            for number in range(6):
                arrived(rp.at[number], first_r + 2 + number)

        return wait

    def to_all(which, name, src_of, dst, dynamic=True):
        first_s, first_r = slots(0, NP), slots(1, NP)
        for by in range(1, NP):
            peer = lax.rem(which + by, NP)
            finish.append(push(
                src_of(peer), dst.at[which], first_s + by, first_r + which, {name: peer}
            ))

        def wait():
            for by in range(1, NP):
                peer = lax.rem(which + by, NP)
                arrived(dst.at[peer], first_r + peer)

        return wait

    pl.semaphore_wait(barrier, 3 * (NP - 1) + 4)
    wait_x = send_halo(main_x, pack_x, 4, rm_x, rp_x)

    tap_row = lax.broadcasted_iota(jnp.int32, (9 * CH, CH), 0)
    tap_col = lax.broadcasted_iota(jnp.int32, (9 * CH, CH), 1)
    fold = (tap_row % CH == tap_col).astype(F32).astype(BF16)
    fold_t = (
        lax.broadcasted_iota(jnp.int32, (CH, 9 * CH), 1) % CH == lax.broadcasted_iota(jnp.int32, (CH, 9 * CH), 0)
    ).astype(F32).astype(BF16)
    eye = (
        lax.broadcasted_iota(jnp.int32, (CH, CH), 0) == lax.broadcasted_iota(jnp.int32, (CH, CH), 1)
    ).astype(F32)
    fetches[1].wait()
    summed = jnp.dot(w_ref[0], fold, preferred_element_type=F32)
    summed_t = lax.dot_general(fold_t, w_ref[0], (((1,), (1,)), ((), ())), preferred_element_type=F32)
    amap[...] = jnp.concatenate(split3(eye + step_size * summed), axis=1)
    atmap[...] = jnp.concatenate(split3(eye + step_size * summed_t), axis=1)
    wait_a = to_all(layer, "layer", lambda peer: amap, ga)
    wait_c = to_all(layer, "layer", lambda peer: x0.at[peer], gc)
    ga[layer] = amap[...]
    gat[layer] = atmap[...]
    gc[layer] = x0[layer]

    block_ok = ((row > 0).astype(F32), None, (row < NP - 1).astype(F32))
    lane_in_row = lax.broadcasted_iota(jnp.int32, (1, 128), 1) % 16
    side_ok = jnp.where(lane_in_row < HALO, (col > 0).astype(F32), (col < NP - 1).astype(F32))
    lane_at = lax.broadcasted_iota(jnp.int32, (CH, 128), 1)
    lane_bf = lane_at.astype(F32).astype(BF16)
    lane16_bf = (lane_at % 16).astype(F32).astype(BF16)
    last_lane, first_lane = lane_bf == 127, lane_bf == 0
    left_end, right_end = lane16_bf == HALO - 1, lane16_bf == HALO
    o_row = lax.broadcasted_iota(jnp.int32, (128, TR * TC), 0)
    o_lane = lax.broadcasted_iota(jnp.int32, (128, TR * TC), 1)
    outward = (((o_lane % TC == 0) & (o_row == o_lane // TC * 16 + 7)) | ((o_lane % TC == 127) & (o_row == o_lane // TC * 16 + 8))).astype(F32).astype(BF16)
    pick0 = (lane_at == 0).astype(F32).astype(BF16)
    pick1 = (lane_at == 127).astype(F32).astype(BF16)
    keep0 = (lane_at != 0).astype(F32).astype(BF16)
    keep1 = (lane_at != 127).astype(F32).astype(BF16)
    on_left = lane_at % 16 < HALO
    for number in range(LG):
        for r in range(3):
            wall[number, r * CH : (r + 1) * CH, :] = w_ref[number, :, r * 192 : (r + 1) * 192]

    def assemble(ref, tile, rm, rp, halo):
        sides = ((2, 3), (0, 1), (4, 5))
        for line in range(HALO - halo, HALO + TR + halo):
            block, r = line // TR, line % TR
            main = tile[r] if block == 1 else rm[block // 2, :, r * TC : (r + 1) * TC].astype(F32)
            ref[:, line * TC : (line + 1) * TC] = main
        for block, (left, right) in enumerate(sides):
            start = MAIN + block * 128
            ref[:, start : start + 128] = jnp.where(on_left, rp[left].astype(F32), rp[right].astype(F32))

    def spread(take, dst, low, high):
        def put(start, values):
            for s, value in enumerate(values):
                dst[s * CH : (s + 1) * CH, start : start + 128] = value

        for block in range(BLOCKS):
            ok = block_ok[block]
            side = take(MAIN + block * 128) * side_ok
            side = (side if ok is None else side * ok).astype(BF16)
            crossing = jnp.zeros((CH, 128), BF16)
            arounds = jnp.dot(side, outward, preferred_element_type=F32).astype(BF16)
            for r in range(TR):
                line = block * TR + r
                if not low <= line < high:
                    continue
                main = take(line * TC)
                main = (main if ok is None else main * ok).astype(BF16)
                put(
                    line * TC,
                    (
                        pltpu.roll(main, 1, 1) * keep0 + arounds[:, r * 128 : (r + 1) * 128] * pick0,
                        main,
                        pltpu.roll(main, 127, 1) * keep1 + arounds[:, r * 128 : (r + 1) * 128] * pick1,
                    ),
                )
                beside = pltpu.roll(main, (16 * r + 8) % 128, 1)
                here = (lane_bf == 16 * r + 7) | (lane_bf == 16 * r + 8)
                crossing = jnp.where(here, beside, crossing)
            put(
                MAIN + block * 128,
                (
                    pltpu.roll(jnp.where(left_end, crossing, side), 1, 1),
                    side,
                    pltpu.roll(jnp.where(right_end, crossing, side), 127, 1),
                ),
            )

    def multiply(matrix, src, low, high):
        for start, size in chunks(low * TC, high * TC, 256) + chunks(MAIN, LEN, 256):
            yw[:, start : start + size] = jnp.dot(matrix, src[:, start : start + size], preferred_element_type=F32)

    def gathered(low, high):
        for start, size in chunks(low * TC, high * TC, 256):
            yield (
                start,
                size,
                yw[:CH, start - TC : start - TC + size]
                + yw[CH : 2 * CH, start : start + size]
                + yw[2 * CH :, start + TC : start + TC + size],
            )
        yield (
            MAIN,
            SIDE,
            pltpu.roll(yw[:CH, MAIN:], 16, 1) + yw[CH : 2 * CH, MAIN:] + pltpu.roll(yw[2 * CH :, MAIN:], SIDE - 16, 1),
        )

    def forward(number, cols, slopes, halo):
        low, high = HALO - halo, HALO + TR + halo
        spread(lambda start: xw[:, start : start + 128], cols, low - 1, high + 1)
        multiply(wall[number], cols, low - 1, high + 1)
        for start, size, total in gathered(low, high):
            bent = jnp.tanh(total)
            xw[:, start : start + size] += step_size * bent
            if slopes is not None:
                slopes[:, start : start + size] = step_size * (1.0 - bent * bent)

    def tile_row(ref, r):
        return ref[:, (HALO + r) * TC : (HALO + r + 1) * TC]

    wait_x()
    assemble(xw, x0, rm_x, rp_x, 4)
    for number in range(LG):
        forward(number, sa.at[0], None, LG - 1 - number)
    for r in range(TR):
        fb[r] = (tile_row(xw, r) - x0[r]).astype(BF16)
    wait_f = to_all(layer, "layer", lambda peer: fb.at[peer], gf)
    gf[layer] = fb[layer]
    fetches[2].wait()
    for r in range(TR):
        value = q_in[0, :, r, :]
        q0[r] = value
        main_q[:, r * TC : (r + 1) * TC] = value.astype(BF16)
    pack_edges(main_q, pack_q)
    wait_q = send_halo(main_q, pack_q, 4, rm_q, rp_q)

    sw[...] = jnp.zeros_like(sw)
    same = (
        lax.broadcasted_iota(jnp.int32, (3 * CH, 3 * CH), 0) == lax.broadcasted_iota(jnp.int32, (3 * CH, 3 * CH), 1)
    ).astype(F32).astype(BF16)
    for number in range(LG):
        for r in range(3):
            turned = lax.dot_general(
                same, wall[number, r * CH : (r + 1) * CH, :], (((1,), (1,)), ((), ())), preferred_element_type=F32
            )
            wback[number, (2 - r) * CH : (3 - r) * CH, :] = jnp.concatenate(
                [turned[2 * CH :], turned[CH : 2 * CH], turned[:CH]], axis=1
            ).astype(BF16)
    wait_a()
    wait_c()
    wait_f()

    def sweep(first, last, by, moves, guesses, maps, out, land, rest=None, rest_land=None):
        first_s, first_r = slots(0, NP), slots(1, NP)
        rest_s, rest_r = slots(0, NP), slots(1, NP)

        def hand(k, src, dst, s_at, r_at):
            @pl.when(layer != k)
            def _():
                push(src.at[k], dst.at[layer], s_at + k, r_at + layer, {"layer": k})

            @pl.when(layer == k)
            def _():
                dst[layer] = src[k]

        offset = None
        for k in range(first, last, by):
            change = moves[k].astype(F32) + (guesses[k] - guesses[k + by])
            if offset is not None:
                high, low = split3(offset)
                wide = maps[k]
                change += jnp.dot(
                    jnp.concatenate([wide, wide[:, :CH]], axis=1),
                    jnp.concatenate([high, high, low], axis=0),
                    preferred_element_type=F32,
                )
            offset = change
            high, low = split3(guesses[k + by] + offset)
            out[k + by] = high
            if rest is not None:
                rest[k + by] = low
            hand(k + by, out, land, first_s, first_r)
        if rest is not None:
            for k in range(first + by, last + by, by):
                hand(k, rest, rest_land, rest_s, rest_r)

        def wait(dst=land, r_at=first_r):
            @pl.when(layer != first)
            def _():
                for step in range(1, NP):
                    peer = lax.rem(layer + step, NP)
                    arrived(dst.at[peer], r_at + peer)

        def wait_rest():
            wait(rest_land, rest_r)

        def done():
            for src, dst, s_at, r_at in ((out, land, first_s, first_r), (rest, rest_land, rest_s, rest_r)):
                if src is None:
                    continue
                for k in range(first + by, last + by, by):

                    @pl.when(layer != k)
                    def _():
                        pltpu.make_async_remote_copy(
                            src_ref=src.at[k], dst_ref=dst.at[layer], send_sem=send.at[s_at + k],
                            recv_sem=recv.at[r_at + layer], device_id={"layer": k}, device_id_type=MESH,
                        ).wait_send()

        return wait, wait_rest, done

    wait_d, wait_rest, done_d = sweep(0, NP - 1, 1, gf, gc, ga, db, rd, dl, rl)

    @pl.when(layer == 0)
    def _():
        for r in range(TR):
            rd[r], rl[r] = split3(x0[r])

    wait_d()
    for r in range(TR):
        main_n[:, r * TC : (r + 1) * TC] = rd[r]
    pack_edges(main_n, pack_n)
    wait_n = send_halo(main_n, pack_n, TR, rm_n, rp_n)
    wait_at = to_all(layer, "layer", lambda peer: atmap, gat)
    wait_cq = to_all(layer, "layer", lambda peer: q0.at[peer], gq)
    gq[layer] = q0[layer]
    wait_rest()
    for r in range(TR):
        value = jnp.where(layer == 0, x0[r], rd[r].astype(F32) + rl[r].astype(F32))
        n0[r] = value
        ns_ref[0, :, r, :] = value
    stores = [pltpu.make_async_copy(ns_ref, ns_hbm, fetch.at[3])]
    stores[0].start()
    wait_q()
    assemble(qw, q0, rm_q, rp_q, 4)

    wait_n()
    assemble(xw, n0, rm_n, rp_n, HALO)
    for number in range(LG):
        forward(number, sa.at[number], ts.at[number], 2 * LG - 1 - number)

    first_s_rr, first_r_rr = slots(0, NP), slots(1, NP)

    for number in reversed(range(LG)):
        low, high = HALO - number, HALO + TR + number
        slopes = ts.at[number]
        spread(lambda start: qw[:, start : start + 128] * slopes[:, start : start + 128], ss, low - 1, high + 1)
        for r in range(3):
            start = r * TC
            sw[r * CH : (r + 1) * CH, start : start + TR * TC] = ss[CH : 2 * CH, HALO * TC : (HALO + TR) * TC]
        grad = lax.dot_general(
            sw[...], sa[number, :, (HALO - 1) * TC : (HALO + TR + 1) * TC], (((1,), (1,)), ((), ())),
            preferred_element_type=F32,
        )
        packed = jnp.concatenate(
            [grad[:, :128], jnp.concatenate([grad[:96, 128:192], grad[96:, 128:192]], axis=1)], axis=0
        )
        for half in range(2):
            piece = 2 * number + half
            gpf[piece] = packed[half * PIECE : (half + 1) * PIECE]
            gpb[piece] = packed[half * PIECE : (half + 1) * PIECE].astype(BF16)

            @pl.when(row != piece)
            def _():
                push(gpb.at[piece], rr.at[row], first_s_rr + piece, first_r_rr + row, {"row": piece})

        multiply(wback[number], ss, low - 1, high + 1)
        for start, size, total in gathered(low, high):
            qw[:, start : start + size] += total

    for r in range(TR):
        gb[r] = (tile_row(qw, r) - q0[r]).astype(BF16)
    wait_g = to_all(layer, "layer", lambda peer: gb.at[peer], gg)
    gg[layer] = gb[layer]
    total = gpf[row]
    for by in range(1, NP):
        peer = lax.rem(row + by, NP)
        arrived(rr.at[peer], first_r_rr + peer)
        total += rr[peer].astype(F32)
    for k in range(NP + 1):
        hb[k] = total[16 * k : 16 * (k + 1)].astype(BF16)
    wait_share = to_all(col, "col", lambda peer: hb.at[peer], share)
    wait_rest = to_all(col, "col", lambda peer: hb.at[NP], common)
    share[col] = hb[col]
    common[col] = hb[NP]

    def added(parts):
        sum_of = parts[0].astype(F32)
        for k in range(1, NP):
            sum_of += parts[k].astype(F32)
        return sum_of.astype(BF16)

    wait_share()
    mine[...] = added(share)
    wait_mine = to_all(col, "col", lambda peer: mine, joined)
    joined[col] = mine[...]
    wait_at()
    wait_cq()
    wait_g()
    wait_e, _, done_e = sweep(NP - 1, 0, -1, gg, gq, gat, eb, re)

    wait_rest()
    wait_mine()
    pb[NP] = added(common)
    for k in range(NP):
        pb[k] = joined[k]
    wait_all = to_all(row, "row", lambda peer: pb, gall)
    gall[row] = pb[...]
    @pl.when(layer == NP - 1)
    def _():
        for r in range(TR):
            na_ref[0, :, r, :] = q0[r]

    @pl.when(layer != NP - 1)
    def _():
        wait_e()
        for r in range(TR):
            na_ref[0, :, r, :] = re[r].astype(F32)

    stores.append(pltpu.make_async_copy(na_ref, na_hbm, fetch.at[4]))
    stores[1].start()

    wait_all()
    for number in range(LG):
        packed = jnp.concatenate(
            [gall[2 * number + half, k] for half in range(2) for k in range(NP + 1)], axis=0
        ).astype(F32)
        rest = jnp.concatenate([packed[192:, :64], packed[192:, 64:]], axis=0)
        for r in range(3):
            wg_ref[number, :, r * 192 : (r + 1) * 192] = jnp.concatenate(
                [packed[r * CH : (r + 1) * CH], rest[r * CH : (r + 1) * CH]], axis=1
            )
        stores.append(pltpu.make_async_copy(wg_ref.at[number], wg_hbm.at[number], fetch.at[5 + number]))
        stores[-1].start()

    for copy in stores:
        copy.wait()
    for copy in finish:
        copy.wait_send()
    done_d()
    done_e()
    for piece in range(NP):

        @pl.when(row != piece)
        def _():
            pltpu.make_async_remote_copy(
                src_ref=gpb.at[piece], dst_ref=rr.at[row], send_sem=send.at[first_s_rr + piece],
                recv_sem=recv.at[first_r_rr + row], device_id={"row": piece}, device_id_type=MESH,
            ).wait_send()


def place_results(*refs):
    sources, results, held, arrive, leave = refs[:3], refs[3:6], refs[6:9], refs[9], refs[10]
    reads = [pltpu.make_async_copy(sources[k], held[k], arrive.at[k]) for k in range(3)]
    writes = [pltpu.make_async_copy(held[k], results[k], leave.at[k]) for k in range(3)]
    for copy in reads:
        copy.start()
    for read, write in zip(reads, writes):
        read.wait()
        write.start()
    for copy in writes:
        copy.wait()


def local(c_states, c_adjoints, weights):
    vm = pltpu.VMEM
    tile = (TR, CH, TC)
    flat = (CH, TR * TC)
    scratch = [
        vm(c_states.shape, F32), vm(c_states.shape, F32), vm(weights.shape, F32),
        vm(c_states.shape, F32), vm(c_states.shape, F32), vm(weights.shape, BF16),
        vm(tile, F32), vm(tile, F32), vm(tile, F32),
        vm(flat, BF16), vm((CH, 128), BF16), vm(flat, BF16), vm((CH, 128), BF16), vm(flat, BF16), vm((CH, 128), BF16),
        vm((2,) + flat, BF16), vm((6, CH, 128), BF16), vm((2,) + flat, BF16), vm((6, CH, 128), BF16),
        vm((2,) + flat, BF16), vm((6, CH, 128), BF16),
        vm((CH, 128), BF16), vm((CH, 128), BF16), vm((NP, CH, 128), BF16), vm((NP, CH, 128), BF16),
        vm(tile, F32), vm(tile, F32), vm(tile, BF16), vm(tile, BF16), vm(tile, BF16), vm(tile, BF16), vm(tile, BF16), vm(tile, BF16),
        vm(tile, BF16), vm(tile, BF16), vm(tile, BF16), vm(tile, BF16),
        vm((LG, 3 * CH, 3 * CH), BF16), vm((LG, 3 * CH, 3 * CH), BF16),
        vm((CH, LEN), F32), vm((CH, LEN), F32),
        vm((3 * CH, LEN), F32), vm((LG, 3 * CH, LEN), BF16), vm((LG, CH, LEN), F32),
        vm((3 * CH, LEN), BF16), vm((3 * CH, (TR + 2) * TC), BF16),
        vm((NP, PIECE, 128), F32), vm((NP, PIECE, 128), BF16), vm((NP, PIECE, 128), BF16),
        vm((NP + 1, 16, 128), BF16), vm((NP, 16, 128), BF16), vm((NP, 16, 128), BF16), vm((16, 128), BF16),
        vm((NP, 16, 128), BF16), vm((NP + 1, 16, 128), BF16), vm((NP, NP + 1, 16, 128), BF16),
        pltpu.SemaphoreType.DMA((160,)), pltpu.SemaphoreType.DMA((160,)), pltpu.SemaphoreType.DMA((5 + LG,)),
    ]
    results = pl.pallas_call(
        body,
        out_shape=(
            jax.ShapeDtypeStruct(c_states.shape, F32),
            jax.ShapeDtypeStruct(c_states.shape, F32),
            jax.ShapeDtypeStruct(weights.shape, F32),
        ),
        in_specs=[pl.BlockSpec(memory_space=pltpu.HBM)] * 3,
        out_specs=[pl.BlockSpec(memory_space=pltpu.HBM)] * 3,
        scratch_shapes=scratch,
        compiler_params=pltpu.CompilerParams(
            collective_id=0, has_side_effects=True, vmem_limit_bytes=60 * 1024 * 1024
        ),
    )(c_states, c_adjoints, weights)
    return pl.pallas_call(
        place_results,
        out_shape=tuple(jax.ShapeDtypeStruct(value.shape, F32) for value in results),
        in_specs=[pl.BlockSpec(memory_space=pltpu.HBM)] * 3,
        out_specs=[pl.BlockSpec(memory_space=pltpu.HBM)] * 3,
        scratch_shapes=[pltpu.VMEM(value.shape, F32) for value in results] + [pltpu.SemaphoreType.DMA((3,))] * 2,
        compiler_params=pltpu.CompilerParams(vmem_limit_bytes=60 * 1024 * 1024),
    )(*results)


def solution(mesh):
    placed = (P("layer", None, "row", "col"), P("layer", None, "row", "col"), P("layer", None, None))
    return jax.shard_map(local, mesh=mesh, in_specs=placed, out_specs=placed, check_vma=False)
```

```python
import functools

import jax
import jax.numpy as jnp
from jax import lax
from jax.experimental import pallas as pl
from jax.experimental.pallas import tpu as pltpu
from jax.sharding import PartitionSpec as P

MESH = pl.DeviceIdType.MESH
F32 = jnp.float32
BF16 = jnp.bfloat16

CH = 64
LG = 4
TR = 8
TC = 128
NP = 8
HALO = 8
RW = TR + 2 * HALO
MAIN = RW * TC
SIDE = RW * 2 * HALO
LEN = MAIN + SIDE
BLOCKS = RW // TR
NEAR = ((0, -1), (0, 1), (-1, -1), (-1, 1), (1, -1), (1, 1))
PIECE = 144
step_size = 0.2


def chunks(low, high, size):
    return [(at, min(size, high - at)) for at in range(low, high, size)]


def split3(matrix):
    high = matrix.astype(BF16)
    low = (matrix - high.astype(F32)).astype(BF16)
    return high, low


def body(
    x_hbm, q_hbm, w_hbm,
    ns_hbm, na_hbm, wg_hbm,
    ns_ref, na_ref, wg_ref, x_in, q_in, w_ref, x0, q0, n0, main_x, pack_x, main_q, pack_q, main_n, pack_n,
    rm_x, rp_x, rm_q, rp_q, rm_n, rp_n,
    amap, atmap, ga, gat, gc, gq, fb, gf, db, rd, dl, rl, gb, gg, eb, re,
    wall, wback, xw, qw, yw, sa, ts, ss, sw,
    gpf, gpb, rr, hb, share, common, mine, joined, pb, gall,
    send, recv, fetch,
):
    layer, row, col = (lax.axis_index(name) for name in ("layer", "row", "col"))
    finish = []
    counter = [0, 0]

    def slots(kind, count):
        first = counter[kind]
        counter[kind] += count
        return first

    def at(which, axis_name, by):
        return {axis_name: lax.rem(which + by + NP, NP)}

    def push(src, dst, send_at, recv_at, device):
        copy = pltpu.make_async_remote_copy(
            src_ref=src, dst_ref=dst, send_sem=send.at[send_at], recv_sem=recv.at[recv_at],
            device_id=device, device_id_type=MESH,
        )
        copy.start()
        return copy

    def arrived(dst, recv_at):
        pltpu.make_async_remote_copy(
            src_ref=dst, dst_ref=dst, send_sem=send.at[0], recv_sem=recv.at[recv_at],
            device_id={"layer": layer}, device_id_type=MESH,
        ).wait_recv()

    fetches = [
        pltpu.make_async_copy(src, dst, fetch.at[number])
        for number, (src, dst) in enumerate(((x_hbm, x_in), (w_hbm, w_ref), (q_hbm, q_in)))
    ]
    for copy in fetches:
        copy.start()

    barrier = pltpu.get_barrier_semaphore()
    for by in range(1, NP):
        for which, name in ((layer, "layer"), (row, "row"), (col, "col")):
            pl.semaphore_signal(barrier, inc=1, device_id=at(which, name, by), device_id_type=MESH)
    for down, right in NEAR[2:]:
        pl.semaphore_signal(
            barrier, inc=1, device_id=at(row, "row", down) | at(col, "col", right), device_id_type=MESH
        )

    spot = lax.broadcasted_iota(jnp.int32, (TR * TC, 128), 0)
    lane = lax.broadcasted_iota(jnp.int32, (TR * TC, 128), 1)
    column, line = spot % TC, spot // TC
    wanted = jnp.where(lane % 16 < HALO, TC - HALO + lane % 16, lane % 16 - HALO)
    picks = (lane // 16 == line) & (column == wanted)
    edges = picks.astype(F32).astype(BF16)

    def pack_edges(main, pack):
        pack[...] = jnp.dot(main[...], edges, preferred_element_type=F32).astype(BF16)

    fetches[0].wait()
    for r in range(TR):
        value = x_in[0, :, r, :]
        x0[r] = value
        main_x[:, r * TC : (r + 1) * TC] = value.astype(BF16)
    pack_edges(main_x, pack_x)

    def send_halo(main, pack, rows, rm, rp):
        first_s, first_r = slots(0, 8), slots(1, 8)
        width = rows * TC
        top, bottom = main.at[:, pl.ds(0, width)], main.at[:, pl.ds((TR - rows) * TC, width)]
        finish.append(push(
            bottom, rm.at[0, :, pl.ds((TR - rows) * TC, width)], first_s, first_r, at(row, "row", 1)
        ))
        finish.append(push(top, rm.at[1, :, pl.ds(0, width)], first_s + 1, first_r + 1, at(row, "row", -1)))
        for number, (down, right) in enumerate(NEAR):
            there = NEAR.index((-down, -right))
            device = at(col, "col", right)
            if down:
                device = device | at(row, "row", down)
            finish.append(push(pack, rp.at[there], first_s + 2 + number, first_r + 2 + there, device))

        def wait():
            arrived(rm.at[0, :, pl.ds((TR - rows) * TC, width)], first_r)
            arrived(rm.at[1, :, pl.ds(0, width)], first_r + 1)
            for number in range(6):
                arrived(rp.at[number], first_r + 2 + number)

        return wait

    def to_all(which, name, src_of, dst, dynamic=True):
        first_s, first_r = slots(0, NP), slots(1, NP)
        for by in range(1, NP):
            peer = lax.rem(which + by, NP)
            finish.append(push(
                src_of(peer), dst.at[which], first_s + by, first_r + which, {name: peer}
            ))

        def wait():
            for by in range(1, NP):
                peer = lax.rem(which + by, NP)
                arrived(dst.at[peer], first_r + peer)

        def wait_one(peer):
            @pl.when(which != peer)
            def _():
                arrived(dst.at[peer], first_r + peer)

        wait.one = wait_one
        return wait

    pl.semaphore_wait(barrier, 3 * (NP - 1) + 4)
    wait_x = send_halo(main_x, pack_x, 4, rm_x, rp_x)

    tap_row = lax.broadcasted_iota(jnp.int32, (9 * CH, CH), 0)
    tap_col = lax.broadcasted_iota(jnp.int32, (9 * CH, CH), 1)
    fold = (tap_row % CH == tap_col).astype(F32).astype(BF16)
    fold_t = (
        lax.broadcasted_iota(jnp.int32, (CH, 9 * CH), 1) % CH == lax.broadcasted_iota(jnp.int32, (CH, 9 * CH), 0)
    ).astype(F32).astype(BF16)
    eye = (
        lax.broadcasted_iota(jnp.int32, (CH, CH), 0) == lax.broadcasted_iota(jnp.int32, (CH, CH), 1)
    ).astype(F32)
    fetches[1].wait()
    summed = jnp.dot(w_ref[0], fold, preferred_element_type=F32)
    summed_t = lax.dot_general(fold_t, w_ref[0], (((1,), (1,)), ((), ())), preferred_element_type=F32)
    amap[...] = jnp.concatenate(split3(eye + step_size * summed), axis=1)
    atmap[...] = jnp.concatenate(split3(eye + step_size * summed_t), axis=1)
    wait_a = to_all(layer, "layer", lambda peer: amap, ga)
    wait_c = to_all(layer, "layer", lambda peer: x0.at[peer], gc)
    ga[layer] = amap[...]
    gat[layer] = atmap[...]
    gc[layer] = x0[layer]

    block_ok = ((row > 0).astype(F32), None, (row < NP - 1).astype(F32))
    lane_in_row = lax.broadcasted_iota(jnp.int32, (1, 128), 1) % 16
    side_ok = jnp.where(lane_in_row < HALO, (col > 0).astype(F32), (col < NP - 1).astype(F32))
    lane_at = lax.broadcasted_iota(jnp.int32, (CH, 128), 1)
    lane_bf = lane_at.astype(F32).astype(BF16)
    lane16_bf = (lane_at % 16).astype(F32).astype(BF16)
    last_lane, first_lane = lane_bf == 127, lane_bf == 0
    left_end, right_end = lane16_bf == HALO - 1, lane16_bf == HALO
    o_row = lax.broadcasted_iota(jnp.int32, (128, TR * TC), 0)
    o_lane = lax.broadcasted_iota(jnp.int32, (128, TR * TC), 1)
    outward = (((o_lane % TC == 0) & (o_row == o_lane // TC * 16 + 7)) | ((o_lane % TC == 127) & (o_row == o_lane // TC * 16 + 8))).astype(F32).astype(BF16)
    pick0 = (lane_at == 0).astype(F32).astype(BF16)
    pick1 = (lane_at == 127).astype(F32).astype(BF16)
    keep0 = (lane_at != 0).astype(F32).astype(BF16)
    keep1 = (lane_at != 127).astype(F32).astype(BF16)
    on_left = lane_at % 16 < HALO
    for number in range(LG):
        for r in range(3):
            wall[number, r * CH : (r + 1) * CH, :] = w_ref[number, :, r * 192 : (r + 1) * 192]

    def assemble(ref, tile, rm, rp, halo):
        sides = ((2, 3), (0, 1), (4, 5))
        for line in range(HALO - halo, HALO + TR + halo):
            block, r = line // TR, line % TR
            main = tile[r] if block == 1 else rm[block // 2, :, r * TC : (r + 1) * TC].astype(F32)
            ref[:, line * TC : (line + 1) * TC] = main
        for block, (left, right) in enumerate(sides):
            start = MAIN + block * 128
            ref[:, start : start + 128] = jnp.where(on_left, rp[left].astype(F32), rp[right].astype(F32))

    def spread(take, dst, low, high):
        def put(start, values):
            for s, value in enumerate(values):
                dst[s * CH : (s + 1) * CH, start : start + 128] = value

        for block in range(BLOCKS):
            ok = block_ok[block]
            side = take(MAIN + block * 128) * side_ok
            side = (side if ok is None else side * ok).astype(BF16)
            crossing = jnp.zeros((CH, 128), BF16)
            arounds = jnp.dot(side, outward, preferred_element_type=F32).astype(BF16)
            for r in range(TR):
                line = block * TR + r
                if not low <= line < high:
                    continue
                main = take(line * TC)
                main = (main if ok is None else main * ok).astype(BF16)
                put(
                    line * TC,
                    (
                        pltpu.roll(main, 1, 1) * keep0 + arounds[:, r * 128 : (r + 1) * 128] * pick0,
                        main,
                        pltpu.roll(main, 127, 1) * keep1 + arounds[:, r * 128 : (r + 1) * 128] * pick1,
                    ),
                )
                beside = pltpu.roll(main, (16 * r + 8) % 128, 1)
                here = (lane_bf == 16 * r + 7) | (lane_bf == 16 * r + 8)
                crossing = jnp.where(here, beside, crossing)
            put(
                MAIN + block * 128,
                (
                    pltpu.roll(jnp.where(left_end, crossing, side), 1, 1),
                    side,
                    pltpu.roll(jnp.where(right_end, crossing, side), 127, 1),
                ),
            )

    def multiply(matrix, src, low, high):
        for start, size in chunks(low * TC, high * TC, 256) + chunks(MAIN, LEN, 256):
            yw[:, start : start + size] = jnp.dot(matrix, src[:, start : start + size], preferred_element_type=F32)

    def gathered(low, high):
        for start, size in chunks(low * TC, high * TC, 256):
            yield (
                start,
                size,
                yw[:CH, start - TC : start - TC + size]
                + yw[CH : 2 * CH, start : start + size]
                + yw[2 * CH :, start + TC : start + TC + size],
            )
        yield (
            MAIN,
            SIDE,
            pltpu.roll(yw[:CH, MAIN:], 16, 1) + yw[CH : 2 * CH, MAIN:] + pltpu.roll(yw[2 * CH :, MAIN:], SIDE - 16, 1),
        )

    def forward(number, cols, slopes, halo):
        low, high = HALO - halo, HALO + TR + halo
        spread(lambda start: xw[:, start : start + 128], cols, low - 1, high + 1)
        multiply(wall[number], cols, low - 1, high + 1)
        for start, size, total in gathered(low, high):
            bent = jnp.tanh(total)
            xw[:, start : start + size] += step_size * bent
            if slopes is not None:
                slopes[:, start : start + size] = step_size * (1.0 - bent * bent)

    def tile_row(ref, r):
        return ref[:, (HALO + r) * TC : (HALO + r + 1) * TC]

    wait_x()
    assemble(xw, x0, rm_x, rp_x, 4)
    for number in range(LG):
        forward(number, sa.at[0], None, LG - 1 - number)
    for r in range(TR):
        fb[r] = (tile_row(xw, r) - x0[r]).astype(BF16)
    wait_f = to_all(layer, "layer", lambda peer: fb.at[peer], gf)
    gf[layer] = fb[layer]
    fetches[2].wait()
    for r in range(TR):
        value = q_in[0, :, r, :]
        q0[r] = value
        main_q[:, r * TC : (r + 1) * TC] = value.astype(BF16)
    pack_edges(main_q, pack_q)
    wait_q = send_halo(main_q, pack_q, 4, rm_q, rp_q)

    sw[...] = jnp.zeros_like(sw)
    same = (
        lax.broadcasted_iota(jnp.int32, (3 * CH, 3 * CH), 0) == lax.broadcasted_iota(jnp.int32, (3 * CH, 3 * CH), 1)
    ).astype(F32).astype(BF16)
    for number in range(LG):
        for r in range(3):
            turned = lax.dot_general(
                same, wall[number, r * CH : (r + 1) * CH, :], (((1,), (1,)), ((), ())), preferred_element_type=F32
            )
            wback[number, (2 - r) * CH : (3 - r) * CH, :] = jnp.concatenate(
                [turned[2 * CH :], turned[CH : 2 * CH], turned[:CH]], axis=1
            ).astype(BF16)
    wait_a()
    wait_c()
    wait_f()

    def sweep(first, last, by, moves, guesses, maps, out, land, rest=None, rest_land=None):
        first_s, first_r = slots(0, NP), slots(1, NP)
        rest_s, rest_r = slots(0, NP), slots(1, NP)

        def hand(k, src, dst, s_at, r_at):
            @pl.when(layer != k)
            def _():
                push(src.at[k], dst.at[layer], s_at + k, r_at + layer, {"layer": k})

            @pl.when(layer == k)
            def _():
                dst[layer] = src[k]

        offset = None
        for k in range(first, last, by):
            change = moves[k].astype(F32) + (guesses[k] - guesses[k + by])
            if offset is not None:
                high, low = split3(offset)
                wide = maps[k]
                change += jnp.dot(
                    jnp.concatenate([wide, wide[:, :CH]], axis=1),
                    jnp.concatenate([high, high, low], axis=0),
                    preferred_element_type=F32,
                )
            offset = change
            high, low = split3(guesses[k + by] + offset)
            out[k + by] = high
            if rest is not None:
                rest[k + by] = low
            hand(k + by, out, land, first_s, first_r)
        if rest is not None:
            for k in range(first + by, last + by, by):
                hand(k, rest, rest_land, rest_s, rest_r)

        def wait(dst=land, r_at=first_r):
            @pl.when(layer != first)
            def _():
                for step in range(1, NP):
                    peer = lax.rem(layer + step, NP)
                    arrived(dst.at[peer], r_at + peer)

        def wait_rest():
            wait(rest_land, rest_r)

        def done():
            for src, dst, s_at, r_at in ((out, land, first_s, first_r), (rest, rest_land, rest_s, rest_r)):
                if src is None:
                    continue
                for k in range(first + by, last + by, by):

                    @pl.when(layer != k)
                    def _():
                        pltpu.make_async_remote_copy(
                            src_ref=src.at[k], dst_ref=dst.at[layer], send_sem=send.at[s_at + k],
                            recv_sem=recv.at[r_at + layer], device_id={"layer": k}, device_id_type=MESH,
                        ).wait_send()

        return wait, wait_rest, done

    wait_d, wait_rest, done_d = sweep(0, NP - 1, 1, gf, gc, ga, db, rd, dl, rl)

    @pl.when(layer == 0)
    def _():
        for r in range(TR):
            rd[r], rl[r] = split3(x0[r])

    wait_d()
    for r in range(TR):
        main_n[:, r * TC : (r + 1) * TC] = rd[r]
    pack_edges(main_n, pack_n)
    wait_n = send_halo(main_n, pack_n, TR, rm_n, rp_n)
    wait_at = to_all(layer, "layer", lambda peer: atmap, gat)
    wait_cq = to_all(layer, "layer", lambda peer: q0.at[peer], gq)
    gq[layer] = q0[layer]
    wait_rest()
    for r in range(TR):
        value = jnp.where(layer == 0, x0[r], rd[r].astype(F32) + rl[r].astype(F32))
        n0[r] = value
        ns_ref[0, :, r, :] = value
    stores = [pltpu.make_async_copy(ns_ref, ns_hbm, fetch.at[3])]
    stores[0].start()
    wait_q()
    assemble(qw, q0, rm_q, rp_q, 4)

    wait_n()
    assemble(xw, n0, rm_n, rp_n, HALO)
    for number in range(LG):
        forward(number, sa.at[number], ts.at[number], 2 * LG - 1 - number)

    first_s_rr, first_r_rr = slots(0, NP), slots(1, NP)

    for number in reversed(range(LG)):
        low, high = HALO - number, HALO + TR + number
        slopes = ts.at[number]
        spread(lambda start: qw[:, start : start + 128] * slopes[:, start : start + 128], ss, low - 1, high + 1)
        for r in range(3):
            start = r * TC
            sw[r * CH : (r + 1) * CH, start : start + TR * TC] = ss[CH : 2 * CH, HALO * TC : (HALO + TR) * TC]
        grad = lax.dot_general(
            sw[...], sa[number, :, (HALO - 1) * TC : (HALO + TR + 1) * TC], (((1,), (1,)), ((), ())),
            preferred_element_type=F32,
        )
        packed = jnp.concatenate(
            [grad[:, :128], jnp.concatenate([grad[:96, 128:192], grad[96:, 128:192]], axis=1)], axis=0
        )
        for half in range(2):
            piece = 2 * number + half
            gpf[piece] = packed[half * PIECE : (half + 1) * PIECE]
            gpb[piece] = packed[half * PIECE : (half + 1) * PIECE].astype(BF16)

            @pl.when(row != piece)
            def _():
                push(gpb.at[piece], rr.at[row], first_s_rr + piece, first_r_rr + row, {"row": piece})

        multiply(wback[number], ss, low - 1, high + 1)
        for start, size, total in gathered(low, high):
            qw[:, start : start + size] += total

    for r in range(TR):
        gb[r] = (tile_row(qw, r) - q0[r]).astype(BF16)
    wait_g = to_all(layer, "layer", lambda peer: gb.at[peer], gg)
    gg[layer] = gb[layer]
    total = gpf[row]
    for by in range(1, NP):
        peer = lax.rem(row + by, NP)
        arrived(rr.at[peer], first_r_rr + peer)
        total += rr[peer].astype(F32)
    for k in range(NP + 1):
        hb[k] = total[16 * k : 16 * (k + 1)].astype(BF16)
    wait_share = to_all(col, "col", lambda peer: hb.at[peer], share)
    wait_rest = to_all(col, "col", lambda peer: hb.at[NP], common)
    share[col] = hb[col]
    common[col] = hb[NP]

    def added(parts):
        sum_of = parts[0].astype(F32)
        for k in range(1, NP):
            sum_of += parts[k].astype(F32)
        return sum_of.astype(BF16)

    wait_at()
    wait_cq()
    wait_g()
    wait_e, _, done_e = sweep(NP - 1, 0, -1, gg, gq, gat, eb, re)

    wait_share()
    mine[...] = added(share)
    wait_mine = to_all(col, "col", lambda peer: mine, joined)
    joined[col] = mine[...]
    wait_rest()
    wait_mine()
    pb[NP] = added(common)
    for k in range(NP):
        pb[k] = joined[k]
    wait_all = to_all(row, "row", lambda peer: pb, gall)
    gall[row] = pb[...]
    @pl.when(layer == NP - 1)
    def _():
        for r in range(TR):
            na_ref[0, :, r, :] = q0[r]

    @pl.when(layer != NP - 1)
    def _():
        wait_e()
        for r in range(TR):
            na_ref[0, :, r, :] = re[r].astype(F32)

    stores.append(pltpu.make_async_copy(na_ref, na_hbm, fetch.at[4]))
    stores[1].start()

    for number in reversed(range(LG)):
        for half in range(2):
            wait_all.one(2 * number + half)
        packed = jnp.concatenate(
            [gall[2 * number + half, k] for half in range(2) for k in range(NP + 1)], axis=0
        ).astype(F32)
        rest = jnp.concatenate([packed[192:, :64], packed[192:, 64:]], axis=0)
        for r in range(3):
            wg_ref[number, :, r * 192 : (r + 1) * 192] = jnp.concatenate(
                [packed[r * CH : (r + 1) * CH], rest[r * CH : (r + 1) * CH]], axis=1
            )
        stores.append(pltpu.make_async_copy(wg_ref.at[number], wg_hbm.at[number], fetch.at[5 + number]))
        stores[-1].start()

    for copy in stores:
        copy.wait()
    for copy in finish:
        copy.wait_send()
    done_d()
    done_e()
    for piece in range(NP):

        @pl.when(row != piece)
        def _():
            pltpu.make_async_remote_copy(
                src_ref=gpb.at[piece], dst_ref=rr.at[row], send_sem=send.at[first_s_rr + piece],
                recv_sem=recv.at[first_r_rr + row], device_id={"row": piece}, device_id_type=MESH,
            ).wait_send()


def place_results(*refs):
    sources, results, held, arrive, leave = refs[:3], refs[3:6], refs[6:9], refs[9], refs[10]
    reads = [pltpu.make_async_copy(sources[k], held[k], arrive.at[k]) for k in range(3)]
    writes = [pltpu.make_async_copy(held[k], results[k], leave.at[k]) for k in range(3)]
    for copy in reads:
        copy.start()
    for read, write in zip(reads, writes):
        read.wait()
        write.start()
    for copy in writes:
        copy.wait()


def local(c_states, c_adjoints, weights):
    vm = pltpu.VMEM
    tile = (TR, CH, TC)
    flat = (CH, TR * TC)
    scratch = [
        vm(c_states.shape, F32), vm(c_states.shape, F32), vm(weights.shape, F32),
        vm(c_states.shape, F32), vm(c_states.shape, F32), vm(weights.shape, BF16),
        vm(tile, F32), vm(tile, F32), vm(tile, F32),
        vm(flat, BF16), vm((CH, 128), BF16), vm(flat, BF16), vm((CH, 128), BF16), vm(flat, BF16), vm((CH, 128), BF16),
        vm((2,) + flat, BF16), vm((6, CH, 128), BF16), vm((2,) + flat, BF16), vm((6, CH, 128), BF16),
        vm((2,) + flat, BF16), vm((6, CH, 128), BF16),
        vm((CH, 128), BF16), vm((CH, 128), BF16), vm((NP, CH, 128), BF16), vm((NP, CH, 128), BF16),
        vm(tile, F32), vm(tile, F32), vm(tile, BF16), vm(tile, BF16), vm(tile, BF16), vm(tile, BF16), vm(tile, BF16), vm(tile, BF16),
        vm(tile, BF16), vm(tile, BF16), vm(tile, BF16), vm(tile, BF16),
        vm((LG, 3 * CH, 3 * CH), BF16), vm((LG, 3 * CH, 3 * CH), BF16),
        vm((CH, LEN), F32), vm((CH, LEN), F32),
        vm((3 * CH, LEN), F32), vm((LG, 3 * CH, LEN), BF16), vm((LG, CH, LEN), F32),
        vm((3 * CH, LEN), BF16), vm((3 * CH, (TR + 2) * TC), BF16),
        vm((NP, PIECE, 128), F32), vm((NP, PIECE, 128), BF16), vm((NP, PIECE, 128), BF16),
        vm((NP + 1, 16, 128), BF16), vm((NP, 16, 128), BF16), vm((NP, 16, 128), BF16), vm((16, 128), BF16),
        vm((NP, 16, 128), BF16), vm((NP + 1, 16, 128), BF16), vm((NP, NP + 1, 16, 128), BF16),
        pltpu.SemaphoreType.DMA((160,)), pltpu.SemaphoreType.DMA((160,)), pltpu.SemaphoreType.DMA((5 + LG,)),
    ]
    results = pl.pallas_call(
        body,
        out_shape=(
            jax.ShapeDtypeStruct(c_states.shape, F32),
            jax.ShapeDtypeStruct(c_states.shape, F32),
            jax.ShapeDtypeStruct(weights.shape, F32),
        ),
        in_specs=[pl.BlockSpec(memory_space=pltpu.HBM)] * 3,
        out_specs=[pl.BlockSpec(memory_space=pltpu.HBM)] * 3,
        scratch_shapes=scratch,
        compiler_params=pltpu.CompilerParams(
            collective_id=0, has_side_effects=True, vmem_limit_bytes=60 * 1024 * 1024
        ),
    )(c_states, c_adjoints, weights)
    return pl.pallas_call(
        place_results,
        out_shape=tuple(jax.ShapeDtypeStruct(value.shape, F32) for value in results),
        in_specs=[pl.BlockSpec(memory_space=pltpu.HBM)] * 3,
        out_specs=[pl.BlockSpec(memory_space=pltpu.HBM)] * 3,
        scratch_shapes=[pltpu.VMEM(value.shape, F32) for value in results] + [pltpu.SemaphoreType.DMA((3,))] * 2,
        compiler_params=pltpu.CompilerParams(vmem_limit_bytes=60 * 1024 * 1024),
    )(*results)


def solution(mesh):
    placed = (P("layer", None, "row", "col"), P("layer", None, "row", "col"), P("layer", None, None))
    return jax.shard_map(local, mesh=mesh, in_specs=placed, out_specs=placed, check_vma=False)
```
